32 devices in a mesh: groups: 2 (over y), ctx: 16 (over z, x, core).
Axes of the slice: x: 2, y: 2, z: 4, core: 2. Of those that a mesh axis runs over, the one named last changes fastest.
Arguments:
- query_vectors: bfloat16 [16384, 2048], P(('groups', 'ctx')), parts along dimension 0, may hold values from -60 to 60
- key_vectors: bfloat16 [16384, 2048], P(('groups', 'ctx')), parts along dimension 0, may hold values from -6 to 6
- value_vectors: bfloat16 [16384, 2048], P(('groups', 'ctx')), parts along dimension 0, may hold values from -8 to 8
- out_weight: bfloat16 [2048, 2048], P(None, 'ctx'), may hold values from -0.125 to 0.125
Outputs:
- projected: bfloat16 [16384, 2048], P(('groups', 'ctx')), parts along dimension 0
The draws below stay inside these ranges and needn't reach their ends.
There are 2 independent parts, one for each index of `groups`. The reference program is written for one: setup_inputs(seed, part) draws one part's arguments, and reference() takes and returns one part's arrays. A program takes and returns all parts, laid end to end along the dimension named above; an argument that names none is the same for every part. Nothing has to cross between parts.
All inputs are finite; a program needn't handle non-finite values.
Results may differ from the reference program's by a relative error of at most 0.0095.
Values may be sent and summed in bfloat16 or wider, within the bound.
A program may use at most 192 MiB of HBM per device.

```python
import math
import jax
import jax.numpy as jnp
from jax import lax

HEADS = 16
HEAD_DIM = 128
WIDTH = 2048
BLOCK = 128
LEVELS = 5
TOKENS = 8192


def query_key_pair(key):
    base_key = jax.random.fold_in(key, 4321)
    key_query = jax.random.fold_in(base_key, 0)
    key_key = jax.random.fold_in(base_key, 1)
    key_qperiod = jax.random.fold_in(base_key, 5)
    key_qphase = jax.random.fold_in(base_key, 6)
    key_kperiod = jax.random.fold_in(base_key, 7)
    key_kphase = jax.random.fold_in(base_key, 8)
    channels = HEADS * HEAD_DIM
    grid_shape = (TOKENS, channels)
    places = jnp.arange(TOKENS, dtype=jnp.float32)[:, None]
    query_period = jnp.exp(jax.random.uniform(key_qperiod, (1, channels), jnp.float32, math.log(1024.0), math.log(16384.0)))
    query_phase = jax.random.uniform(key_qphase, (1, channels), jnp.float32, -math.pi, math.pi)
    key_period = jnp.exp(jax.random.uniform(key_kperiod, (1, channels), jnp.float32, math.log(256.0), math.log(2048.0)))
    key_phase = jax.random.uniform(key_kphase, (1, channels), jnp.float32, -math.pi, math.pi)
    query_wave = 3.0 * jnp.sin(2.0 * math.pi * places / query_period + query_phase)
    key_wave = 1.5 * jnp.sin(2.0 * math.pi * places / key_period + key_phase)
    key_rows = jnp.clip(jax.random.normal(key_key, grid_shape, jnp.float32), -4.5, 4.5) + key_wave
    query_rows = 2.0 * jnp.clip(jax.random.normal(key_query, grid_shape, jnp.float32), -6.0, 6.0) + query_wave
    return (query_rows, key_rows)


def draw_query_vectors(key, part):
    return query_key_pair(key)[0].astype(jnp.bfloat16)


def draw_key_vectors(key, part):
    return query_key_pair(key)[1].astype(jnp.bfloat16)


def draw_value_vectors(key, part):
    key_rough, key_period, key_phase, key_coarse = jax.random.split(jax.random.fold_in(key, 8765), 4)
    channels = HEADS * HEAD_DIM
    grid_shape = (TOKENS, channels)
    coarse_shape = (TOKENS // 8, channels)
    rough = jnp.clip(jax.random.normal(key_rough, grid_shape, jnp.float32), -6.0, 6.0)
    coarse = 2.5 * jnp.clip(jax.random.normal(key_coarse, coarse_shape, jnp.float32), -3.0, 3.0)
    period = jnp.exp(jax.random.uniform(key_period, (1, channels), jnp.float32, math.log(TOKENS / 16.0), math.log(TOKENS / 2.0)))
    phase = jax.random.uniform(key_phase, (1, channels), jnp.float32, -math.pi, math.pi)
    places = jnp.arange(TOKENS, dtype=jnp.float32)[:, None]
    total = rough + jnp.repeat(coarse, 8, axis=0) + 1.5 * jnp.sin(2.0 * math.pi * places / period + phase)
    return jnp.clip(total, -8.0, 8.0).astype(jnp.bfloat16)


def level_of(stream_key, shape, cuts, smallest, top_value):
    loudness, own = 1.0, jax.random.fold_in(stream_key, 6)
    for axis_at, parts in cuts:
        steps = jnp.exp(jax.random.uniform(jax.random.fold_in(own, axis_at), (parts,), jnp.float32, smallest / len(cuts), top_value / len(cuts)))
        loudness = loudness * jnp.repeat(steps, shape[axis_at] // parts).reshape([-1 if axis == axis_at else 1 for axis in range(len(shape))])
    return loudness


def scatter_about(rng, dims, width, limit, pieces=(), held_as=jnp.bfloat16):
    array = jax.random.normal(rng, dims, jnp.float32) * width
    if len(pieces) > 0:
        array = level_of(rng, dims, pieces, -0.22, 0.18) * array
    return jnp.clip(array, min=-limit, max=limit).astype(held_as)


def setup_inputs(seed: int = 0, part: int = 0) -> dict:
    seeds = jax.random.split(jax.random.key(seed), 5)
    own_keys = jax.random.split(jax.random.fold_in(seeds[4], part), 5)
    query_vectors = draw_query_vectors(jax.random.fold_in(jax.random.fold_in(seeds[4], part), 71), part)
    key_vectors = draw_key_vectors(jax.random.fold_in(jax.random.fold_in(seeds[4], part), 71), part)
    value_vectors = draw_value_vectors(jax.random.fold_in(jax.random.fold_in(seeds[4], part), 71), part)
    out_weight = scatter_about(seeds[3], (HEADS * HEAD_DIM, WIDTH), (HEADS * HEAD_DIM) ** -0.5, 0.125, ((1, 16),))
    return dict(query_vectors=query_vectors, key_vectors=key_vectors, value_vectors=value_vectors, out_weight=out_weight)


def coarsen(matrix):
    paired = matrix.reshape(matrix.shape[0] // 2, 2, matrix.shape[1]).astype(jnp.float32)
    return ((paired[:, 0] + paired[:, 1]) * 0.5).astype(jnp.bfloat16)


def key_valid(height, block_index, row_pos, nblocks):
    grid_shape = (block_index.shape[0], row_pos.shape[0], BLOCK)
    has_left = jnp.broadcast_to((block_index >= 1)[:, None, None], grid_shape)
    has_right = jnp.broadcast_to((block_index + 1 < nblocks)[:, None, None], grid_shape)
    if height == 0:
        return jnp.concatenate([has_left, jnp.ones(grid_shape, jnp.bool_), has_right], axis=2)
    upper_half = (row_pos >= BLOCK // 2)[None, :, None]
    key_place = jnp.arange(BLOCK, dtype=jnp.int32)[None, None, :]
    left_ok = has_left & (upper_half | (key_place < BLOCK // 2))
    right_ok = has_right & (jnp.logical_not(upper_half) | (key_place >= BLOCK // 2))
    return jnp.concatenate([left_ok, right_ok], axis=2)


def level_terms(height, query_rows, key_rows, value_rows):
    score_scale = HEAD_DIM ** -0.5
    nblocks = query_rows.shape[0] // BLOCK
    zero_block = jnp.zeros((1, BLOCK, HEADS, HEAD_DIM), jnp.bfloat16)
    query_blocks = query_rows.reshape(nblocks, BLOCK, HEADS, HEAD_DIM)
    key_padded = jnp.concatenate([zero_block, key_rows.reshape(nblocks, BLOCK, HEADS, HEAD_DIM), zero_block], axis=0)
    value_padded = jnp.concatenate([zero_block, value_rows.reshape(nblocks, BLOCK, HEADS, HEAD_DIM), zero_block], axis=0)
    row_pos = jnp.arange(BLOCK, dtype=jnp.int32)

    def one_block(block_no):
        near_keys = lax.dynamic_slice_in_dim(key_padded, block_no, 3, 0)
        near_values = lax.dynamic_slice_in_dim(value_padded, block_no, 3, 0)
        if height == 0:
            keys_window = near_keys.reshape(3 * BLOCK, HEADS, HEAD_DIM)
            values_window = near_values.reshape(3 * BLOCK, HEADS, HEAD_DIM)
        else:
            keys_window = jnp.concatenate([near_keys[0], near_keys[2]], axis=0)
            values_window = jnp.concatenate([near_values[0], near_values[2]], axis=0)
        admitted = key_valid(height, block_no[None], row_pos, nblocks)[0][None]
        queries = query_blocks[block_no]
        scores = jnp.einsum("rhd,khd->hrk", queries.astype(jnp.float32), keys_window.astype(jnp.float32),
                            precision=lax.Precision.HIGHEST) * score_scale
        scores = jnp.where(admitted, scores, -jnp.inf)
        row_peak = jnp.max(scores, axis=2)
        weights = jnp.where(admitted, jnp.exp(scores - row_peak[:, :, None]), 0.0).astype(jnp.bfloat16)
        numerator = jnp.einsum("hrk,khd->rhd", weights.astype(jnp.float32), values_window.astype(jnp.float32),
                               precision=lax.Precision.HIGHEST)
        denominator = jnp.sum(weights.astype(jnp.float32), axis=2)
        return row_peak.T, numerator, denominator.T

    return lax.map(one_block, jnp.arange(nblocks, dtype=jnp.int32))


def merge_levels(peaks, numerators, denominators):
    spread = [jnp.repeat(peaks[height], 1 << height, axis=0) for height in range(len(peaks))]
    highest = spread[0]
    for level_peak in spread[1:]:
        highest = jnp.maximum(highest, level_peak)
    weighted = 0.0
    normaliser = 0.0
    for height in range(len(peaks)):
        factor = float(1 << height) * jnp.exp(spread[height] - highest)
        weighted = weighted + factor[:, :, None] * jnp.repeat(numerators[height], 1 << height, axis=0)
        normaliser = normaliser + factor * jnp.repeat(denominators[height], 1 << height, axis=0)
    return weighted / normaliser[:, :, None]


def reference(query_vectors, key_vectors, value_vectors, out_weight):
    length = query_vectors.shape[0]
    query_rows, key_rows, value_rows = query_vectors, key_vectors, value_vectors
    peaks, numerators, denominators = [], [], []
    for height in range(LEVELS):
        if height > 0:
            query_rows = coarsen(query_rows)
            key_rows = coarsen(key_rows)
            value_rows = coarsen(value_rows)
        row_peak, numerator, denominator = level_terms(height, query_rows, key_rows, value_rows)
        coarse_rows = length >> height
        peaks.append(row_peak.reshape(coarse_rows, HEADS))
        numerators.append(numerator.reshape(coarse_rows, HEADS, HEAD_DIM))
        denominators.append(denominator.reshape(coarse_rows, HEADS))
    attended = merge_levels(peaks, numerators, denominators).astype(jnp.bfloat16).reshape(length, HEADS * HEAD_DIM)
    return jnp.dot(attended, out_weight, preferred_element_type=jnp.float32).astype(jnp.bfloat16)
```

```python
import functools
import math

import jax
import jax.numpy as jnp
from jax import lax
from jax.experimental import pallas as pl
from jax.experimental.pallas import tpu as pltpu
from jax.sharding import PartitionSpec as P

HEADS = 16
HEAD_DIM = 128
BLOCK = 128
HALF = BLOCK // 2
BF16 = jnp.bfloat16
F32 = jnp.float32
RATE = HEAD_DIM ** (-0.5) * math.log2(math.e)
MASKED = -1e30


def pool(rows):
    count = rows.shape[0] // 2
    at = lax.broadcasted_iota(jnp.int32, (count, 2 * count), 0)
    source = lax.broadcasted_iota(jnp.int32, (count, 2 * count), 1)
    half = jnp.where((source >> 1) == at, 0.5, 0.0).astype(BF16)
    return jnp.dot(half, rows, preferred_element_type=F32).astype(BF16)


def messages_kernel(k_ref, v_ref, right_ref, left_ref, third_ref, fourth_ref):
    for which, ref in enumerate((k_ref, v_ref)):
        rows = ref[...]
        first = pool(rows)
        second = pool(first)
        third = pool(second)
        right_ref[which, 0:128] = rows[384:512]
        right_ref[which, 128:192] = first[128:192]
        right_ref[which, 192:256] = second[0:64]
        left_ref[which, 0:128] = rows[0:128]
        left_ref[which, 128:192] = first[64:128]
        left_ref[which, 192:256] = second[64:128]
        third_ref[which] = third
        fourth_ref[which] = pool(third)


def make_messages(keys, values):
    width = keys.shape[1]
    cols = 512
    shapes = [256, 256, 64, 32]
    return pl.pallas_call(
        messages_kernel,
        grid=(width // cols,),
        in_specs=[pl.BlockSpec((512, cols), lambda j: (0, j))] * 2,
        out_specs=[pl.BlockSpec((2, n, cols), lambda j: (0, 0, j)) for n in shapes],
        out_shape=[jax.ShapeDtypeStruct((2, n, width), BF16) for n in shapes],
        compiler_params=pltpu.CompilerParams(vmem_limit_bytes=40 << 20),
        name="messages",
    )(keys, values)


def attend(queries, keys, values, bias=None):
    scores = lax.dot_general(queries, keys, (((1,), (1,)), ((), ())), preferred_element_type=F32)
    if bias is not None:
        scores = scores + bias
    peak = jnp.max(scores, axis=1, keepdims=True)
    weights = jnp.exp2((scores - peak) * RATE).astype(BF16)
    ones = jnp.ones((values.shape[0], HEAD_DIM), BF16)
    both = jnp.dot(weights, jnp.concatenate([values, ones], axis=1), preferred_element_type=F32)
    return (
        jnp.broadcast_to(peak, (queries.shape[0], HEAD_DIM)),
        both[:, :HEAD_DIM],
        both[:, HEAD_DIM:],
    )


def stack(parts):
    return tuple(jnp.concatenate(items, axis=0) for items in zip(*parts))


def merged(height, fine, coarse, scratch):
    rows = fine[0].shape[0]
    spread = []
    for which, part in enumerate(coarse):
        scratch[which, pl.ds(0, rows // 2, stride=2), :] = part
        scratch[which, pl.ds(1, rows // 2, stride=2), :] = part
        spread.append(scratch[which, pl.ds(0, rows), :])
    top = jnp.maximum(fine[0], spread[0])
    here = jnp.exp2((fine[0] - top) * RATE) * float(1 << height)
    there = jnp.exp2((spread[0] - top) * RATE)
    return (top, here * fine[1] + there * spread[1], here * fine[2] + there * spread[2])


def bias_row(pieces):
    total = sum(count for count, _ in pieces)
    lane = lax.broadcasted_iota(jnp.int32, (1, total), 1)
    row = jnp.zeros((1, total), F32)
    start = 0
    for count, allowed in pieces:
        if allowed is not None:
            inside = (lane >= start) & (lane < start + count)
            row = jnp.where(inside, jnp.where(allowed, 0.0, MASKED), row)
        start += count
    return row


def edge_flags(height, position, ctx_size):
    span = max(1, (1 << height) // 4)
    block = position // span
    return block >= 1, block + 1 < ctx_size // span


def head_attention(position, ctx_size, q, kv, left, right, thirds, fourths, scratch):
    k_of = lambda x: x[:, :HEAD_DIM]
    v_of = lambda x: x[:, HEAD_DIM:]
    everything = jnp.concatenate([kv, q], axis=1)
    levels = [everything]
    for _ in range(4):
        levels.append(pool(levels[-1]))
    q_at = [level[:, 2 * HEAD_DIM :] for level in levels]
    kv_at = [level[:, : 2 * HEAD_DIM] for level in levels]

    left0, left1b = left[0:128], left[128:192]
    right0, right1b = right[0:128], right[128:192]
    left1 = jnp.concatenate([left1b, pool(left0)], axis=0)
    right1 = jnp.concatenate([pool(right0), right1b], axis=0)
    left2 = jnp.concatenate([left[192:256], pool(left1)], axis=0)
    right2 = jnp.concatenate([pool(right1), right[192:256]], axis=0)

    def window(queries, pieces):
        rows = jnp.concatenate([piece for piece, _ in pieces], axis=0)
        bias = None
        if any(allowed is not None for _, allowed in pieces):
            bias = bias_row([(piece.shape[0], allowed) for piece, allowed in pieces])
        return attend(queries, k_of(rows), v_of(rows), bias)

    def halves(queries, before, has_before, after, has_after):
        return [
            window(queries[:HALF], [(before[:HALF], has_before), (after, has_after)]),
            window(queries[HALF:], [(before, has_before), (after[HALF:], has_after)]),
        ]

    has_left, has_right = edge_flags(4, position, ctx_size)
    turn = position % 4
    tests = [has_left, has_right]
    from_right = [
        (turn == 1) | (turn == 3),
        (turn == 0) | (turn == 2),
        (turn == 0) | (turn == 1),
        (turn == 0) | (turn == 1),
    ]
    pieces = [(fourths[0], has_left), (fourths[1], has_right)]
    for chunk, is_right in zip(fourths[2:], from_right):
        pieces.append((chunk, (is_right & has_right) | (~is_right & has_left)))
    peak, total, weight = window(q_at[4], pieces)
    state = (peak, total * 16.0, weight * 16.0)

    has_left, has_right = edge_flags(3, position, ctx_size)
    is_right = position % 2 == 0
    mixed = (is_right & has_right) | (~is_right & has_left)
    state = merged(
        3,
        window(
            q_at[3], [(thirds[0], has_left), (thirds[1], has_right), (thirds[2], mixed)]
        ),
        state,
        scratch,
    )

    has_left, has_right = edge_flags(2, position, ctx_size)
    state = merged(2, stack(halves(q_at[2], left2, has_left, right2, has_right)), state, scratch)

    kv1 = kv_at[1]
    state = merged(
        1,
        stack(
            halves(q_at[1][:128], left1, has_left, kv1[128:], None)
            + halves(q_at[1][128:], kv1[:128], None, right1, has_right)
        ),
        state,
        scratch,
    )

    parts = [window(q[0:128], [(left0, has_left), (kv[0:256], None)])]
    for block in (1, 2):
        start = 128 * block
        parts.append(window(q[start : start + 128], [(kv[start - 128 : start + 256], None)]))
    parts.append(window(q[384:512], [(kv[256:512], None), (right0, has_right)]))
    _, total, weight = merged(0, stack(parts), state, scratch)
    return (total / weight).astype(BF16)


def attention_kernel(ctx_size, pos_ref, q_ref, k_ref, v_ref, left_ref, right_ref, *rest):
    chunks, out_ref, scratch = rest[:9], rest[9], rest[10]
    pair = lambda ref: jnp.concatenate([ref[0], ref[1]], axis=1)
    kv = jnp.concatenate([k_ref[...], v_ref[...]], axis=1)
    chunk_rows = [pair(ref) for ref in chunks]
    out_ref[...] = head_attention(
        pos_ref[0],
        ctx_size,
        q_ref[...],
        kv,
        pair(left_ref),
        pair(right_ref),
        chunk_rows[:3],
        chunk_rows[3:],
        scratch,
    )


def attention(ctx_size, position, queries, keys, values, left, right, thirds, fourths):
    rows, width = queries.shape
    own = pl.BlockSpec((rows, HEAD_DIM), lambda h: (0, h))
    beside = lambda n: pl.BlockSpec((2, n, HEAD_DIM), lambda h: (0, 0, h))
    return pl.pallas_call(
        functools.partial(attention_kernel, ctx_size),
        grid=(HEADS,),
        in_specs=[pl.BlockSpec(memory_space=pltpu.SMEM), own, own, own, beside(256), beside(256)]
        + [beside(64)] * 3
        + [beside(32)] * 6,
        out_specs=own,
        out_shape=jax.ShapeDtypeStruct((rows, width), BF16),
        scratch_shapes=[pltpu.VMEM((3, rows, HEAD_DIM), F32)],
        compiler_params=pltpu.CompilerParams(vmem_limit_bytes=40 << 20),
        name="attention",
    )(position[None].astype(jnp.int32), queries, keys, values, left, right, *thirds, *fourths)


def project_kernel(x_ref, w_ref, out_ref):
    weight = jnp.concatenate([w_ref[0], w_ref[1]], axis=1)
    out_ref[...] = jnp.dot(x_ref[...], weight, preferred_element_type=F32).astype(BF16)


def project(attended, shards):
    rows, width = attended.shape
    count, _, cols = shards.shape
    return pl.pallas_call(
        project_kernel,
        grid=(count // 2,),
        in_specs=[
            pl.BlockSpec((rows, width), lambda j: (0, 0)),
            pl.BlockSpec((2, width, cols), lambda j: (j, 0, 0)),
        ],
        out_specs=pl.BlockSpec((rows, 2 * cols), lambda j: (0, j)),
        out_shape=jax.ShapeDtypeStruct((rows, count * cols), BF16),
        compiler_params=pltpu.CompilerParams(vmem_limit_bytes=40 << 20),
        name="project",
    )(attended, shards)


def moved(array, ctx_size, offset_of):
    route = []
    for target in range(ctx_size):
        source = target + offset_of(target)
        if 0 <= source < ctx_size:
            route.append((source, target))
    return lax.ppermute(array, "ctx", route)


THIRD_OFFSETS = [lambda i: -2, lambda i: 2, lambda i: (3, -3)[i % 2]]
FOURTH_OFFSETS = [
    lambda i: -4,
    lambda i: 4,
    lambda i: (-3, 3, -3, 3)[i % 4],
    lambda i: (5, -5, 5, -5)[i % 4],
    lambda i: (6, 6, -6, -6)[i % 4],
    lambda i: (7, 5, -5, -7)[i % 4],
]


def per_device(query_vectors, key_vectors, value_vectors, out_weight):
    ctx_size = lax.axis_size("ctx")
    position = lax.axis_index("ctx")
    whole_shards = out_weight.shape[1] % 128 == 0
    if whole_shards:
        weight = lax.all_gather(out_weight, "ctx", axis=0)
    else:
        weight = lax.all_gather(out_weight, "ctx", axis=1, tiled=True)
    to_right, to_left, third, fourth = make_messages(key_vectors, value_vectors)
    left = moved(to_right, ctx_size, lambda i: -1)
    right = moved(to_left, ctx_size, lambda i: 1)
    thirds = [moved(third, ctx_size, offset) for offset in THIRD_OFFSETS]
    fourths = [moved(fourth, ctx_size, offset) for offset in FOURTH_OFFSETS]
    attended = attention(
        ctx_size, position, query_vectors, key_vectors, value_vectors, left, right, thirds, fourths
    )
    if whole_shards:
        return project(attended, weight)
    return jnp.dot(attended, weight, preferred_element_type=F32).astype(BF16)


def solution(mesh):
    in_specs = (
        P(("groups", "ctx"), None),
        P(("groups", "ctx"), None),
        P(("groups", "ctx"), None),
        P(None, "ctx"),
    )
    out_specs = P(("groups", "ctx"), None)
    return jax.shard_map(
        per_device, mesh=mesh, in_specs=in_specs, out_specs=out_specs, check_vma=False
    )
```

```python
import functools
import math

import jax
import jax.numpy as jnp
from jax import lax
from jax.experimental import pallas as pl
from jax.experimental.pallas import tpu as pltpu
from jax.sharding import PartitionSpec as P

HEADS = 16
HEAD_DIM = 128
BLOCK = 128
HALF = BLOCK // 2
BF16 = jnp.bfloat16
F32 = jnp.float32
RATE = HEAD_DIM ** (-0.5) * math.log2(math.e)
MASKED = -1e30


def pool(rows):
    count = rows.shape[0] // 2
    at = lax.broadcasted_iota(jnp.int32, (count, 2 * count), 0)
    source = lax.broadcasted_iota(jnp.int32, (count, 2 * count), 1)
    half = jnp.where((source >> 1) == at, 0.5, 0.0).astype(BF16)
    return jnp.dot(half, rows, preferred_element_type=F32).astype(BF16)


def attend(queries, keys, values, bias=None):
    scores = lax.dot_general(queries, keys, (((1,), (1,)), ((), ())), preferred_element_type=F32)
    if bias is not None:
        scores = scores + bias
    peak = jnp.max(scores, axis=1, keepdims=True)
    weights = jnp.exp2((scores - peak) * RATE).astype(BF16)
    ones = jnp.ones((values.shape[0], HEAD_DIM), BF16)
    both = jnp.dot(weights, jnp.concatenate([values, ones], axis=1), preferred_element_type=F32)
    return (
        jnp.broadcast_to(peak, (queries.shape[0], HEAD_DIM)),
        both[:, :HEAD_DIM],
        both[:, HEAD_DIM:],
    )


def stack(parts):
    return tuple(jnp.concatenate(items, axis=0) for items in zip(*parts))


def merged(height, fine, coarse, scratch):
    rows = fine[0].shape[0]
    spread = []
    for which, part in enumerate(coarse):
        scratch[which, pl.ds(0, rows // 2, stride=2), :] = part
        scratch[which, pl.ds(1, rows // 2, stride=2), :] = part
        spread.append(scratch[which, pl.ds(0, rows), :])
    top = jnp.maximum(fine[0], spread[0])
    here = jnp.exp2((fine[0] - top) * RATE) * float(1 << height)
    there = jnp.exp2((spread[0] - top) * RATE)
    return (top, here * fine[1] + there * spread[1], here * fine[2] + there * spread[2])


def bias_row(pieces):
    total = sum(count for count, _ in pieces)
    lane = lax.broadcasted_iota(jnp.int32, (1, total), 1)
    row = jnp.zeros((1, total), F32)
    start = 0
    for count, allowed in pieces:
        if allowed is not None:
            inside = (lane >= start) & (lane < start + count)
            row = jnp.where(inside, jnp.where(allowed, 0.0, MASKED), row)
        start += count
    return row


def edge_flags(height, position, ctx_size):
    span = max(1, (1 << height) // 4)
    block = position // span
    return block >= 1, block + 1 < ctx_size // span


def head_attention(position, ctx_size, q, kv, left, right, thirds, fourths, scratch):
    k_of = lambda x: x[:, :HEAD_DIM]
    v_of = lambda x: x[:, HEAD_DIM:]
    everything = jnp.concatenate([kv, q], axis=1)
    levels = [everything]
    for _ in range(4):
        levels.append(pool(levels[-1]))
    q_at = [level[:, 2 * HEAD_DIM :] for level in levels]
    kv_at = [level[:, : 2 * HEAD_DIM] for level in levels]

    left0, left1b = left[0:128], left[128:192]
    right0, right1b = right[0:128], right[128:192]
    left1 = jnp.concatenate([left1b, pool(left0)], axis=0)
    right1 = jnp.concatenate([pool(right0), right1b], axis=0)
    left2 = jnp.concatenate([left[192:256], pool(left1)], axis=0)
    right2 = jnp.concatenate([pool(right1), right[192:256]], axis=0)

    def window(queries, pieces):
        rows = jnp.concatenate([piece for piece, _ in pieces], axis=0)
        bias = None
        if any(allowed is not None for _, allowed in pieces):
            bias = bias_row([(piece.shape[0], allowed) for piece, allowed in pieces])
        return attend(queries, k_of(rows), v_of(rows), bias)

    def halves(queries, before, has_before, after, has_after):
        return [
            window(queries[:HALF], [(before[:HALF], has_before), (after, has_after)]),
            window(queries[HALF:], [(before, has_before), (after[HALF:], has_after)]),
        ]

    has_left, has_right = edge_flags(4, position, ctx_size)
    turn = position % 4
    tests = [has_left, has_right]
    from_right = [
        (turn == 1) | (turn == 3),
        (turn == 0) | (turn == 2),
        (turn == 0) | (turn == 1),
        (turn == 0) | (turn == 1),
    ]
    pieces = [(fourths[0], has_left), (fourths[1], has_right)]
    for chunk, is_right in zip(fourths[2:], from_right):
        pieces.append((chunk, (is_right & has_right) | (~is_right & has_left)))
    peak, total, weight = window(q_at[4], pieces)
    state = (peak, total * 16.0, weight * 16.0)

    has_left, has_right = edge_flags(3, position, ctx_size)
    is_right = position % 2 == 0
    mixed = (is_right & has_right) | (~is_right & has_left)
    state = merged(
        3,
        window(
            q_at[3], [(thirds[0], has_left), (thirds[1], has_right), (thirds[2], mixed)]
        ),
        state,
        scratch,
    )

    has_left, has_right = edge_flags(2, position, ctx_size)
    state = merged(2, stack(halves(q_at[2], left2, has_left, right2, has_right)), state, scratch)

    kv1 = kv_at[1]
    state = merged(
        1,
        stack(
            halves(q_at[1][:128], left1, has_left, kv1[128:], None)
            + halves(q_at[1][128:], kv1[:128], None, right1, has_right)
        ),
        state,
        scratch,
    )

    parts = [window(q[0:128], [(left0, has_left), (kv[0:256], None)])]
    for block in (1, 2):
        start = 128 * block
        parts.append(window(q[start : start + 128], [(kv[start - 128 : start + 256], None)]))
    parts.append(window(q[384:512], [(kv[256:512], None), (right0, has_right)]))
    _, total, weight = merged(0, stack(parts), state, scratch)
    return (total / weight).astype(BF16)


SLOT_OFFSETS = [
    (-1, -1, -1, -1),
    (1, 1, 1, 1),
    (-2, -2, -2, -2),
    (2, 2, 2, 2),
    (3, -3, 3, -3),
    (-4, -4, -4, -4),
    (4, 4, 4, 4),
    (-3, 3, -3, 3),
    (5, -5, 5, -5),
    (6, 6, -6, -6),
    (7, 5, -5, -7),
]
REACH = 7
CHUNKS = 8
CHUNK_HEADS = HEADS // CHUNKS


def by_turn(turn, table):
    value = table[3]
    for at in (2, 1, 0):
        value = jnp.where(turn == at, table[at], value)
    return value


def inverse(table):
    back = [0, 0, 0, 0]
    for turn, offset in enumerate(table):
        back[(turn + offset) % 4] = -offset
    return tuple(back)


def layer_kernel(ctx_size, with_weight, *refs):
    if with_weight:
        q_ref, k_ref, v_ref, w_ref, out_ref = refs[:5]
        refs = refs[5:]
        w_all, w_recv, w_send, w_core = refs[-4:]
    else:
        q_ref, k_ref, v_ref, out_ref = refs[:4]
        refs = refs[4:]
    (to_right, to_left, third, fourth, left, right, thirds, fourths,
     scratch, att, send_sem, recv_sem) = refs[:12]

    position = lax.axis_index("ctx")
    group = lax.axis_index("groups")
    turn = position % 4

    barrier = pltpu.get_barrier_semaphore()
    reach = ctx_size - 1 if with_weight else min(REACH, ctx_size - 1)
    for distance in range(1, reach + 1):
        for offset in (-distance, distance):
            peer = position + offset

            @pl.when((peer >= 0) & (peer < ctx_size))
            def _():
                pl.semaphore_signal(
                    barrier, inc=1, device_id={"ctx": peer}, device_id_type=pl.DeviceIdType.MESH
                )

    peers = jnp.minimum(position, reach) + jnp.minimum(ctx_size - 1 - position, reach)
    if with_weight:
        pl.semaphore_signal(
            barrier, inc=1, device_id={"groups": 1 - group}, device_id_type=pl.DeviceIdType.MESH
        )
        peers = peers + 1

    slots = [left, right] + [thirds.at[i] for i in range(3)] + [fourths.at[i] for i in range(6)]
    sources = [to_right, to_left] + [third] * 3 + [fourth] * 6
    givers = [position + by_turn(turn, table) for table in SLOT_OFFSETS]
    takers = [position + by_turn(turn, inverse(table)) for table in SLOT_OFFSETS]
    inside = lambda peer: (peer >= 0) & (peer < ctx_size)

    pl.semaphore_wait(barrier, peers)

    for slot, giver in zip(slots, givers):

        @pl.when(jnp.logical_not(inside(giver)))
        def _():
            slot[...] = jnp.zeros(slot.shape, BF16)

    def slot_copy(chunk, which):
        heads = pl.ds(chunk * CHUNK_HEADS, CHUNK_HEADS)
        return pltpu.make_async_remote_copy(
            src_ref=sources[which].at[heads],
            dst_ref=slots[which].at[heads],
            send_sem=send_sem.at[chunk, which],
            recv_sem=recv_sem.at[chunk, which],
            device_id={"ctx": takers[which]},
            device_id_type=pl.DeviceIdType.MESH,
        )

    steps = []
    if with_weight:
        z = position // 4
        depth = ctx_size // 4
        partner = position + 2 - 4 * ((position // 2) % 2)
        sibling = position + 1 - 2 * (position % 2)

        def piece(shard, half, send, device):
            return pltpu.make_async_remote_copy(
                src_ref=w_all.at[shard, half],
                dst_ref=w_all.at[shard, half],
                send_sem=send,
                recv_sem=w_recv.at[shard, half],
                device_id=device,
                device_id_type=pl.DeviceIdType.MESH,
            )

        def to_x(shard):
            return piece(shard, group, w_send.at[0, shard], {"ctx": partner})

        def to_z(shard, way):
            kind = 1 if way > 0 else 2
            return piece(shard, group, w_send.at[kind, shard], {"ctx": position + 4 * way})

        def to_y(shard):
            return piece(shard, group, w_send.at[3, shard], {"groups": 1 - group})

        def to_core(shard, half, own):
            send = w_send.at[4, shard] if own else w_core.at[shard]
            return piece(shard, half, send, {"ctx": sibling})

        always = None
        can_go = {1: z + 1 < depth, -1: z >= 1}
        first = [(always, lambda: to_x(position))]
        for way in (1, -1):
            first.append((can_go[way], functools.partial(to_z, position, way)))
        first.append((always, lambda: to_core(position, group, True)))
        first.append((always, lambda: to_core(position, 1 - group, False)))
        steps.append([(always, None, first)])
        second = [(can_go[way], functools.partial(to_z, partner, way)) for way in (1, -1)]
        second.append((always, lambda: to_y(partner)))
        second.append((always, lambda: to_core(partner, group, True)))
        steps.append([(always, (partner, group), second)])
        for hops in range(1, depth):
            step = []
            for way in (1, -1):
                here = (z - hops * way >= 0) & (z - hops * way < depth)
                for base in (position, partner):
                    shard = base - 4 * hops * way
                    sends = [
                        (can_go[way], functools.partial(to_z, shard, way)),
                        (always, functools.partial(to_y, shard)),
                        (always, functools.partial(to_core, shard, group, True)),
                    ]
                    step.append((here, (shard, group), sends))
            steps.append(step)
        step = []
        for turns in range(depth):
            for base in (position, partner):
                if turns == 0 and base is position:
                    continue
                level = lax.rem(z + turns, depth)
                shard = base + 4 * (level - z)
                sends = [(always, functools.partial(to_core, shard, 1 - group, False))]
                step.append((always, (shard, 1 - group), sends))
        steps.append(step)

    def when(condition, action):
        if condition is None:
            action()
        else:
            pl.when(condition)(action)

    def run_step(step):
        for here, awaited, sends in step:

            def act(awaited=awaited, sends=sends):
                if awaited is not None:
                    piece(*awaited, w_core.at[0], {"ctx": sibling}).wait_recv()
                for condition, copy in sends:
                    when(condition, lambda copy=copy: copy().start())

            when(here, act)

    def finish_step(step):
        for here, _, sends in step:

            def act(sends=sends):
                for condition, copy in sends:
                    when(condition, lambda copy=copy: copy().wait_send())

            when(here, act)

    if with_weight:
        w_all[position, 0] = w_ref[0:1024]
        w_all[position, 1] = w_ref[1024:2048]
        run_step(steps[0])

    def prepare(chunk, _):
        cols = CHUNK_HEADS * HEAD_DIM
        lanes = pl.ds(pl.multiple_of(chunk * cols, cols), cols)
        for which, ref in enumerate((k_ref, v_ref)):
            rows = ref[:, lanes]
            first = pool(rows)
            second = pool(first)
            eighth = pool(second)
            sixteenth = pool(eighth)
            for at in range(CHUNK_HEADS):
                head = chunk * CHUNK_HEADS + at
                cut = slice(at * HEAD_DIM, (at + 1) * HEAD_DIM)
                to_right[head, which, 0:128] = rows[384:512, cut]
                to_right[head, which, 128:192] = first[128:192, cut]
                to_right[head, which, 192:256] = second[0:64, cut]
                to_left[head, which, 0:128] = rows[0:128, cut]
                to_left[head, which, 128:192] = first[64:128, cut]
                to_left[head, which, 192:256] = second[64:128, cut]
                third[head, which] = eighth[:, cut]
                fourth[head, which] = sixteenth[:, cut]
        for which, taker in enumerate(takers):
            when(inside(taker), lambda which=which: slot_copy(chunk, which).start())
        return 0

    lax.fori_loop(0, CHUNKS, prepare, 0)
    if with_weight:
        run_step(steps[1])

    def one_head(head, _):
        chunk = head // CHUNK_HEADS

        @pl.when(head % CHUNK_HEADS == 0)
        def _():
            for which, giver in enumerate(givers):
                when(inside(giver), lambda which=which: slot_copy(chunk, which).wait_recv())

        if with_weight:
            for at, step in enumerate(steps[2:]):
                pl.when(head == 1 + 2 * at)(functools.partial(run_step, step))
        lanes = pl.ds(pl.multiple_of(head * HEAD_DIM, HEAD_DIM), HEAD_DIM)
        pair = lambda ref: jnp.concatenate([ref[head, 0], ref[head, 1]], axis=1)
        att[:, lanes] = head_attention(
            position,
            ctx_size,
            q_ref[:, lanes],
            jnp.concatenate([k_ref[:, lanes], v_ref[:, lanes]], axis=1),
            pair(left),
            pair(right),
            [pair(thirds.at[i]) for i in range(3)],
            [pair(fourths.at[i]) for i in range(6)],
            scratch,
        )
        return 0

    lax.fori_loop(0, HEADS, one_head, 0)

    if with_weight:
        for level in range(depth):
            for other in (0, 2):
                for half in range(2):
                    shard = 4 * level + other + 1 - position % 2
                    piece(shard, half, w_core.at[0], {"ctx": sibling}).wait_recv()

        def project(at, _):
            count = 2048
            weight = jnp.concatenate(
                [w_all[2 * at].reshape(count, 128), w_all[2 * at + 1].reshape(count, 128)], axis=1
            )
            result = jnp.dot(att[...], weight, preferred_element_type=F32)
            out_ref[:, pl.ds(pl.multiple_of(at * 256, 256), 256)] = result.astype(BF16)
            return 0

        lax.fori_loop(0, ctx_size // 2, project, 0)
        for step in steps:
            finish_step(step)
    else:
        out_ref[...] = att[...]

    def settle(chunk, _):
        for which, taker in enumerate(takers):
            when(inside(taker), lambda which=which: slot_copy(chunk, which).wait_send())
        return 0

    lax.fori_loop(0, CHUNKS, settle, 0)


def layer(ctx_size, queries, keys, values, weight=None):
    rows, width = queries.shape
    per_head = lambda *lead: pltpu.VMEM((*lead, HEAD_DIM), BF16)
    slots = len(SLOT_OFFSETS)
    scratch = [
        per_head(HEADS, 2, 256),
        per_head(HEADS, 2, 256),
        per_head(HEADS, 2, 64),
        per_head(HEADS, 2, 32),
        per_head(HEADS, 2, 256),
        per_head(HEADS, 2, 256),
        per_head(3, HEADS, 2, 64),
        per_head(6, HEADS, 2, 32),
        pltpu.VMEM((3, rows, HEAD_DIM), F32),
        pltpu.VMEM((rows, width), BF16),
        pltpu.SemaphoreType.DMA((CHUNKS, slots)),
        pltpu.SemaphoreType.DMA((CHUNKS, slots)),
    ]
    operands = [queries, keys, values]
    if weight is not None:
        operands.append(weight)
        scratch += [
            pltpu.VMEM((ctx_size, 2, weight.shape[0] // 2, weight.shape[1]), BF16),
            pltpu.SemaphoreType.DMA((ctx_size, 2)),
            pltpu.SemaphoreType.DMA((5, ctx_size)),
            pltpu.SemaphoreType.DMA((ctx_size,)),
        ]
    return pl.pallas_call(
        functools.partial(layer_kernel, ctx_size, weight is not None),
        in_specs=[pl.BlockSpec(memory_space=pltpu.VMEM)] * len(operands),
        out_specs=pl.BlockSpec(memory_space=pltpu.VMEM),
        out_shape=jax.ShapeDtypeStruct((rows, width), BF16),
        scratch_shapes=scratch,
        compiler_params=pltpu.CompilerParams(
            collective_id=0, has_side_effects=True, vmem_limit_bytes=56 << 20
        ),
        name="layer",
    )(*operands)


def per_device(query_vectors, key_vectors, value_vectors, out_weight):
    ctx_size = lax.axis_size("ctx")
    in_kernel = (
        out_weight.shape[1] == 128 and ctx_size % 4 == 0 and lax.axis_size("groups") == 2
    )
    if in_kernel:
        return layer(ctx_size, query_vectors, key_vectors, value_vectors, out_weight)
    weight = lax.all_gather(out_weight, "ctx", axis=1, tiled=True)
    attended = layer(ctx_size, query_vectors, key_vectors, value_vectors)
    return jnp.dot(attended, weight, preferred_element_type=F32).astype(BF16)


def solution(mesh):
    in_specs = (
        P(("groups", "ctx"), None),
        P(("groups", "ctx"), None),
        P(("groups", "ctx"), None),
        P(None, "ctx"),
    )
    out_specs = P(("groups", "ctx"), None)
    return jax.shard_map(
        per_device, mesh=mesh, in_specs=in_specs, out_specs=out_specs, check_vma=False
    )
```

```python
import functools
import math

import jax
import jax.numpy as jnp
from jax import lax
from jax.experimental import pallas as pl
from jax.experimental.pallas import tpu as pltpu
from jax.sharding import PartitionSpec as P

HEADS = 16
HEAD_DIM = 128
BLOCK = 128
HALF = BLOCK // 2
BF16 = jnp.bfloat16
F32 = jnp.float32
RATE = HEAD_DIM ** (-0.5) * math.log2(math.e)
MASKED = -1e30


def pool(rows):
    count = rows.shape[0] // 2
    at = lax.broadcasted_iota(jnp.int32, (count, 2 * count), 0)
    source = lax.broadcasted_iota(jnp.int32, (count, 2 * count), 1)
    half = jnp.where((source >> 1) == at, 0.5, 0.0).astype(BF16)
    return jnp.dot(half, rows, preferred_element_type=F32).astype(BF16)


def attend(queries, keys, values, bias=None):
    scores = lax.dot_general(queries, keys, (((1,), (1,)), ((), ())), preferred_element_type=F32)
    if bias is not None:
        scores = scores + bias
    peak = jnp.max(scores, axis=1, keepdims=True)
    weights = jnp.exp2((scores - peak) * RATE).astype(BF16)
    ones = jnp.ones((values.shape[0], HEAD_DIM), BF16)
    both = jnp.dot(weights, jnp.concatenate([values, ones], axis=1), preferred_element_type=F32)
    return (
        jnp.broadcast_to(peak, (queries.shape[0], HEAD_DIM)),
        both[:, :HEAD_DIM],
        both[:, HEAD_DIM:],
    )


def stack(parts):
    return tuple(jnp.concatenate(items, axis=0) for items in zip(*parts))


def merged(height, fine, coarse, scratch):
    rows = fine[0].shape[0]
    spread = []
    for which, part in enumerate(coarse):
        scratch[which, pl.ds(0, rows // 2, stride=2), :] = part
        scratch[which, pl.ds(1, rows // 2, stride=2), :] = part
        spread.append(scratch[which, pl.ds(0, rows), :])
    top = jnp.maximum(fine[0], spread[0])
    here = jnp.exp2((fine[0] - top) * RATE) * float(1 << height)
    there = jnp.exp2((spread[0] - top) * RATE)
    return (top, here * fine[1] + there * spread[1], here * fine[2] + there * spread[2])


def bias_row(pieces):
    total = sum(count for count, _ in pieces)
    lane = lax.broadcasted_iota(jnp.int32, (1, total), 1)
    row = jnp.zeros((1, total), F32)
    start = 0
    for count, allowed in pieces:
        if allowed is not None:
            inside = (lane >= start) & (lane < start + count)
            row = jnp.where(inside, jnp.where(allowed, 0.0, MASKED), row)
        start += count
    return row


def edge_flags(height, position, ctx_size):
    span = max(1, (1 << height) // 4)
    block = position // span
    return block >= 1, block + 1 < ctx_size // span


def head_attention(position, ctx_size, q, kv, left, right, thirds, fourths, scratch):
    k_of = lambda x: x[:, :HEAD_DIM]
    v_of = lambda x: x[:, HEAD_DIM:]
    everything = jnp.concatenate([kv, q], axis=1)
    levels = [everything]
    for _ in range(4):
        levels.append(pool(levels[-1]))
    q_at = [level[:, 2 * HEAD_DIM :] for level in levels]
    kv_at = [level[:, : 2 * HEAD_DIM] for level in levels]

    left0, left1b = left[0:128], left[128:192]
    right0, right1b = right[0:128], right[128:192]
    left1 = jnp.concatenate([left1b, pool(left0)], axis=0)
    right1 = jnp.concatenate([pool(right0), right1b], axis=0)
    left2 = jnp.concatenate([left[192:256], pool(left1)], axis=0)
    right2 = jnp.concatenate([pool(right1), right[192:256]], axis=0)

    def window(queries, pieces):
        rows = jnp.concatenate([piece for piece, _ in pieces], axis=0)
        bias = None
        if any(allowed is not None for _, allowed in pieces):
            bias = bias_row([(piece.shape[0], allowed) for piece, allowed in pieces])
        return attend(queries, k_of(rows), v_of(rows), bias)

    def halves(queries, before, has_before, after, has_after):
        return [
            window(queries[:HALF], [(before[:HALF], has_before), (after, has_after)]),
            window(queries[HALF:], [(before, has_before), (after[HALF:], has_after)]),
        ]

    has_left, has_right = edge_flags(4, position, ctx_size)
    is_right = position % 4 < 2
    mixed = (is_right & has_right) | (~is_right & has_left)
    pieces = []
    for chunks in (fourths[:3], fourths[3:]):
        pieces += list(zip(chunks, (has_left, has_right, mixed)))
    peak, total, weight = window(q_at[4], pieces)
    state = (peak, total * 16.0, weight * 16.0)

    has_left, has_right = edge_flags(3, position, ctx_size)
    odd = position % 2 == 1
    own = (odd & has_right) | (~odd & has_left)
    other = (odd & has_left) | (~odd & has_right)
    state = merged(
        3,
        window(q_at[3], [(thirds[0], own), (thirds[1], other), (thirds[2], other)]),
        state,
        scratch,
    )

    has_left, has_right = edge_flags(2, position, ctx_size)
    state = merged(2, stack(halves(q_at[2], left2, has_left, right2, has_right)), state, scratch)

    kv1 = kv_at[1]
    state = merged(
        1,
        stack(
            halves(q_at[1][:128], left1, has_left, kv1[128:], None)
            + halves(q_at[1][128:], kv1[:128], None, right1, has_right)
        ),
        state,
        scratch,
    )

    parts = [window(q[0:128], [(left0, has_left), (kv[0:256], None)])]
    for block in (1, 2):
        start = 128 * block
        parts.append(window(q[start : start + 128], [(kv[start - 128 : start + 256], None)]))
    parts.append(window(q[384:512], [(kv[256:512], None), (right0, has_right)]))
    _, total, weight = merged(0, stack(parts), state, scratch)
    return (total / weight).astype(BF16)


SLOT_OFFSETS = [
    (-1, -1, -1, -1),
    (1, 1, 1, 1),
    (-2, 2, -2, 2),
    (-4, -4, -4, -4),
    (4, 4, 4, 4),
    (6, 6, -6, -6),
]
PASSED = 5
REACH = 7
CHUNKS = 8
CHUNK_HEADS = HEADS // CHUNKS


def by_turn(turn, table):
    value = table[3]
    for at in (2, 1, 0):
        value = jnp.where(turn == at, table[at], value)
    return value


def inverse(table):
    back = [0, 0, 0, 0]
    for turn, offset in enumerate(table):
        back[(turn + offset) % 4] = -offset
    return tuple(back)


def layer_kernel(ctx_size, with_weight, *refs):
    if with_weight:
        q_ref, k_ref, v_ref, w_ref, out_ref = refs[:5]
        refs = refs[5:]
        w_all, w_recv, w_send, w_core = refs[-4:]
    else:
        q_ref, k_ref, v_ref, out_ref = refs[:4]
        refs = refs[4:]
    (to_right, to_left, third, fourth, rims, thirds, fourths, pooled, their_thirds,
     their_pooled, their_fourths, scratch, att, send_sem, recv_sem, pass_send,
     pass_recv) = refs[:17]

    position = lax.axis_index("ctx")
    group = lax.axis_index("groups")
    turn = position % 4

    barrier = pltpu.get_barrier_semaphore()
    reach = ctx_size - 1 if with_weight else min(REACH, ctx_size - 1)
    for distance in range(1, reach + 1):
        for offset in (-distance, distance):
            peer = position + offset

            @pl.when((peer >= 0) & (peer < ctx_size))
            def _():
                pl.semaphore_signal(
                    barrier, inc=1, device_id={"ctx": peer}, device_id_type=pl.DeviceIdType.MESH
                )

    peers = jnp.minimum(position, reach) + jnp.minimum(ctx_size - 1 - position, reach)
    if with_weight:
        pl.semaphore_signal(
            barrier, inc=1, device_id={"groups": 1 - group}, device_id_type=pl.DeviceIdType.MESH
        )
        peers = peers + 1

    slots = [rims.at[0], rims.at[1], thirds] + [fourths.at[i] for i in range(3)]
    sources = [to_right, to_left, third] + [fourth] * 3
    passed = [thirds, pooled] + [fourths.at[i] for i in range(3)]
    passed_to = [their_thirds, their_pooled] + [their_fourths.at[i] for i in range(3)]
    sibling = position + 1 - 2 * (position % 2)
    givers = [position + by_turn(turn, table) for table in SLOT_OFFSETS]
    takers = [position + by_turn(turn, inverse(table)) for table in SLOT_OFFSETS]
    inside = lambda peer: (peer >= 0) & (peer < ctx_size)

    own_there = [inside(giver) for giver in givers]
    across = inside(position + 2 - 4 * (position % 2))
    send_there = [own_there[2], own_there[2]] + own_there[3:]
    pass_there = [across, across] + own_there[3:]

    pl.semaphore_wait(barrier, peers)

    for slot, there in zip(slots + passed_to, own_there + pass_there):

        @pl.when(jnp.logical_not(there))
        def _():
            slot[...] = jnp.zeros(slot.shape, BF16)

    def when(condition, action):
        if condition is None:
            action()
        else:
            pl.when(condition)(action)

    def slot_copy(chunk, which):
        heads = pl.ds(chunk * CHUNK_HEADS, CHUNK_HEADS)
        return pltpu.make_async_remote_copy(
            src_ref=sources[which].at[heads],
            dst_ref=slots[which].at[heads],
            send_sem=send_sem.at[chunk, which],
            recv_sem=recv_sem.at[chunk, which],
            device_id={"ctx": takers[which]},
            device_id_type=pl.DeviceIdType.MESH,
        )

    def pass_copy(chunk, which):
        heads = pl.ds(chunk * CHUNK_HEADS, CHUNK_HEADS)
        return pltpu.make_async_remote_copy(
            src_ref=passed[which].at[heads],
            dst_ref=passed_to[which].at[heads],
            send_sem=pass_send.at[chunk, which],
            recv_sem=pass_recv.at[chunk, which],
            device_id={"ctx": sibling},
            device_id_type=pl.DeviceIdType.MESH,
        )

    def forward(chunk):
        for which, there in enumerate(own_there):
            when(there, lambda which=which: slot_copy(chunk, which).wait_recv())
        lanes = []
        for at in range(CHUNK_HEADS):
            for which in range(2):
                lanes.append(rims[position % 2, chunk * CHUNK_HEADS + at, which])
        rows = jnp.concatenate(lanes, axis=1)
        eighth = jnp.concatenate(
            [pool(rows[192:256]), pool(pool(rows[128:192])), pool(pool(pool(rows[0:128])))], axis=0
        )
        for at in range(CHUNK_HEADS):
            for which in range(2):
                start = (2 * at + which) * HEAD_DIM
                pooled[chunk * CHUNK_HEADS + at, which] = eighth[:, start : start + HEAD_DIM]
        for which, there in enumerate(send_there):
            when(there, lambda which=which: pass_copy(chunk, which).start())

    steps = []
    if with_weight:
        z = position // 4
        depth = ctx_size // 4
        partner = position + 2 - 4 * ((position // 2) % 2)

        def piece(shard, half, send, device):
            return pltpu.make_async_remote_copy(
                src_ref=w_all.at[shard, half],
                dst_ref=w_all.at[shard, half],
                send_sem=send,
                recv_sem=w_recv.at[shard, half],
                device_id=device,
                device_id_type=pl.DeviceIdType.MESH,
            )

        def to_x(shard):
            return piece(shard, group, w_send.at[0, shard], {"ctx": partner})

        def to_z(shard, way):
            kind = 1 if way > 0 else 2
            return piece(shard, group, w_send.at[kind, shard], {"ctx": position + 4 * way})

        def to_y(shard):
            return piece(shard, group, w_send.at[3, shard], {"groups": 1 - group})

        def to_core(shard, half, own):
            send = w_send.at[4, shard] if own else w_core.at[shard]
            return piece(shard, half, send, {"ctx": sibling})

        always = None
        can_go = {1: z + 1 < depth, -1: z >= 1}
        first = [(always, lambda: to_x(position))]
        for way in (1, -1):
            first.append((can_go[way], functools.partial(to_z, position, way)))
        first.append((always, lambda: to_core(position, group, True)))
        first.append((always, lambda: to_core(position, 1 - group, False)))
        steps.append([(always, None, first)])
        second = [(can_go[way], functools.partial(to_z, partner, way)) for way in (1, -1)]
        second.append((always, lambda: to_y(partner)))
        second.append((always, lambda: to_core(partner, group, True)))
        steps.append([(always, (partner, group), second)])
        for hops in range(1, depth):
            step = []
            for way in (1, -1):
                here = (z - hops * way >= 0) & (z - hops * way < depth)
                for base in (position, partner):
                    shard = base - 4 * hops * way
                    sends = [
                        (can_go[way], functools.partial(to_z, shard, way)),
                        (always, functools.partial(to_y, shard)),
                        (always, functools.partial(to_core, shard, group, True)),
                    ]
                    step.append((here, (shard, group), sends))
            steps.append(step)
        step = []
        for turns in range(depth):
            for base in (position, partner):
                if turns == 0 and base is position:
                    continue
                level = lax.rem(z + turns, depth)
                shard = base + 4 * (level - z)
                sends = [(always, functools.partial(to_core, shard, 1 - group, False))]
                step.append((always, (shard, 1 - group), sends))
        steps.append(step)

    def run_step(step):
        for here, awaited, sends in step:

            def act(awaited=awaited, sends=sends):
                if awaited is not None:
                    piece(*awaited, w_core.at[0], {"ctx": sibling}).wait_recv()
                for condition, copy in sends:
                    when(condition, lambda copy=copy: copy().start())

            when(here, act)

    def finish_step(step):
        for here, _, sends in step:

            def act(sends=sends):
                for condition, copy in sends:
                    when(condition, lambda copy=copy: copy().wait_send())

            when(here, act)

    if with_weight:
        w_all[position, 0] = w_ref[0:1024]
        w_all[position, 1] = w_ref[1024:2048]
        run_step(steps[0])

    def prepare(chunk, _):
        cols = CHUNK_HEADS * HEAD_DIM
        lanes = pl.ds(pl.multiple_of(chunk * cols, cols), cols)
        for which, ref in enumerate((k_ref, v_ref)):
            rows = ref[:, lanes]
            first = pool(rows)
            second = pool(first)
            eighth = pool(second)
            sixteenth = pool(eighth)
            for at in range(CHUNK_HEADS):
                head = chunk * CHUNK_HEADS + at
                cut = slice(at * HEAD_DIM, (at + 1) * HEAD_DIM)
                to_right[head, which, 0:128] = rows[384:512, cut]
                to_right[head, which, 128:192] = first[128:192, cut]
                to_right[head, which, 192:256] = second[0:64, cut]
                to_left[head, which, 0:128] = rows[0:128, cut]
                to_left[head, which, 128:192] = first[64:128, cut]
                to_left[head, which, 192:256] = second[64:128, cut]
                third[head, which] = eighth[:, cut]
                fourth[head, which] = sixteenth[:, cut]
        for which, taker in enumerate(takers):
            when(inside(taker), lambda which=which: slot_copy(chunk, which).start())
        return 0

    lax.fori_loop(0, CHUNKS, prepare, 0)
    if with_weight:
        run_step(steps[1])

    def one_head(head, _):
        chunk = head // CHUNK_HEADS

        @pl.when(head == 0)
        def _():
            forward(0)

        @pl.when((head % CHUNK_HEADS == CHUNK_HEADS - 1) & (chunk + 1 < CHUNKS))
        def _():
            forward(chunk + 1)

        @pl.when(head % CHUNK_HEADS == 0)
        def _():
            for which, there in enumerate(pass_there):
                when(there, lambda which=which: pass_copy(chunk, which).wait_recv())

        if with_weight:
            for at, step in enumerate(steps[2:]):
                pl.when(head == 1 + 2 * at)(functools.partial(run_step, step))
        lanes = pl.ds(pl.multiple_of(head * HEAD_DIM, HEAD_DIM), HEAD_DIM)
        pair = lambda ref: jnp.concatenate([ref[head, 0], ref[head, 1]], axis=1)
        att[:, lanes] = head_attention(
            position,
            ctx_size,
            q_ref[:, lanes],
            jnp.concatenate([k_ref[:, lanes], v_ref[:, lanes]], axis=1),
            pair(rims.at[0]),
            pair(rims.at[1]),
            [pair(ref) for ref in (thirds, their_thirds, their_pooled)],
            [pair(ref.at[i]) for ref in (fourths, their_fourths) for i in range(3)],
            scratch,
        )
        return 0

    lax.fori_loop(0, HEADS, one_head, 0)

    if with_weight:
        for level in range(depth):
            for other in (0, 2):
                for half in range(2):
                    shard = 4 * level + other + 1 - position % 2
                    piece(shard, half, w_core.at[0], {"ctx": sibling}).wait_recv()

        def project(at, _):
            count = 2048
            weight = jnp.concatenate(
                [w_all[2 * at].reshape(count, 128), w_all[2 * at + 1].reshape(count, 128)], axis=1
            )
            result = jnp.dot(att[...], weight, preferred_element_type=F32)
            out_ref[:, pl.ds(pl.multiple_of(at * 256, 256), 256)] = result.astype(BF16)
            return 0

        lax.fori_loop(0, ctx_size // 2, project, 0)
        for step in steps:
            finish_step(step)
    else:
        out_ref[...] = att[...]

    def settle(chunk, _):
        for which, taker in enumerate(takers):
            when(inside(taker), lambda which=which: slot_copy(chunk, which).wait_send())
        for which, there in enumerate(send_there):
            when(there, lambda which=which: pass_copy(chunk, which).wait_send())
        return 0

    lax.fori_loop(0, CHUNKS, settle, 0)


def layer(ctx_size, queries, keys, values, weight=None):
    rows, width = queries.shape
    per_head = lambda *lead: pltpu.VMEM((*lead, HEAD_DIM), BF16)
    slots = len(SLOT_OFFSETS)
    scratch = [
        per_head(HEADS, 2, 256),
        per_head(HEADS, 2, 256),
        per_head(HEADS, 2, 64),
        per_head(HEADS, 2, 32),
        per_head(2, HEADS, 2, 256),
        per_head(HEADS, 2, 64),
        per_head(3, HEADS, 2, 32),
        per_head(HEADS, 2, 64),
        per_head(HEADS, 2, 64),
        per_head(HEADS, 2, 64),
        per_head(3, HEADS, 2, 32),
        pltpu.VMEM((3, rows, HEAD_DIM), F32),
        pltpu.VMEM((rows, width), BF16),
        pltpu.SemaphoreType.DMA((CHUNKS, slots)),
        pltpu.SemaphoreType.DMA((CHUNKS, slots)),
        pltpu.SemaphoreType.DMA((CHUNKS, PASSED)),
        pltpu.SemaphoreType.DMA((CHUNKS, PASSED)),
    ]
    operands = [queries, keys, values]
    if weight is not None:
        operands.append(weight)
        scratch += [
            pltpu.VMEM((ctx_size, 2, weight.shape[0] // 2, weight.shape[1]), BF16),
            pltpu.SemaphoreType.DMA((ctx_size, 2)),
            pltpu.SemaphoreType.DMA((5, ctx_size)),
            pltpu.SemaphoreType.DMA((ctx_size,)),
        ]
    return pl.pallas_call(
        functools.partial(layer_kernel, ctx_size, weight is not None),
        in_specs=[pl.BlockSpec(memory_space=pltpu.VMEM)] * len(operands),
        out_specs=pl.BlockSpec(memory_space=pltpu.VMEM),
        out_shape=jax.ShapeDtypeStruct((rows, width), BF16),
        scratch_shapes=scratch,
        compiler_params=pltpu.CompilerParams(
            collective_id=0, has_side_effects=True, vmem_limit_bytes=56 << 20
        ),
        name="layer",
    )(*operands)


def per_device(query_vectors, key_vectors, value_vectors, out_weight):
    ctx_size = lax.axis_size("ctx")
    in_kernel = (
        out_weight.shape[1] == 128 and ctx_size % 4 == 0 and lax.axis_size("groups") == 2
    )
    if in_kernel:
        return layer(ctx_size, query_vectors, key_vectors, value_vectors, out_weight)
    weight = lax.all_gather(out_weight, "ctx", axis=1, tiled=True)
    attended = layer(ctx_size, query_vectors, key_vectors, value_vectors)
    return jnp.dot(attended, weight, preferred_element_type=F32).astype(BF16)


def solution(mesh):
    in_specs = (
        P(("groups", "ctx"), None),
        P(("groups", "ctx"), None),
        P(("groups", "ctx"), None),
        P(None, "ctx"),
    )
    out_specs = P(("groups", "ctx"), None)
    return jax.shard_map(
        per_device, mesh=mesh, in_specs=in_specs, out_specs=out_specs, check_vma=False
    )
```

```python
import functools
import math

import jax
import jax.numpy as jnp
from jax import lax
from jax.experimental import pallas as pl
from jax.experimental.pallas import tpu as pltpu
from jax.sharding import PartitionSpec as P

HEADS = 16
HEAD_DIM = 128
BLOCK = 128
HALF = BLOCK // 2
BF16 = jnp.bfloat16
F32 = jnp.float32
RATE = HEAD_DIM ** (-0.5) * math.log2(math.e)
MASKED = -1e30


def pooling_matrix():
    at = lax.broadcasted_iota(jnp.int32, (BLOCK, 2 * BLOCK), 0)
    source = lax.broadcasted_iota(jnp.int32, (BLOCK, 2 * BLOCK), 1)
    return jnp.where((source >> 1) == at, 0.5, 0.0).astype(BF16)


def pool(rows, halving):
    means = []
    for start in range(0, rows.shape[0], 2 * BLOCK):
        part = rows[start : start + 2 * BLOCK]
        count = part.shape[0]
        half = halving[: count // 2, :count]
        means.append(jnp.dot(half, part, preferred_element_type=F32).astype(BF16))
    return means[0] if len(means) == 1 else jnp.concatenate(means, axis=0)


def raw_scores(queries, keys, _, bias):
    scores = lax.dot_general(queries, keys, (((1,), (1,)), ((), ())), preferred_element_type=F32)
    return scores if bias is None else scores + bias


def softmax_terms(scores, values):
    peak = jnp.max(scores, axis=1, keepdims=True)
    weights = jnp.exp2((scores - peak) * RATE).astype(BF16)
    ones = jnp.ones((values.shape[0], HEAD_DIM), BF16)
    both = jnp.dot(weights, jnp.concatenate([values, ones], axis=1), preferred_element_type=F32)
    return (
        jnp.broadcast_to(peak, (scores.shape[0], HEAD_DIM)),
        both[:, :HEAD_DIM],
        both[:, HEAD_DIM:],
    )


def attend_all(windows):
    ahead = 3
    scores, terms = {}, []
    for at in range(len(windows) + ahead):
        if at < len(windows):
            scores[at] = raw_scores(*windows[at])
        if at >= ahead:
            terms.append(softmax_terms(scores.pop(at - ahead), windows[at - ahead][2]))
    return terms


def stack(parts):
    return tuple(jnp.concatenate(items, axis=0) for items in zip(*parts))


def merged(height, fine, coarse, scratch):
    rows = fine[0].shape[0]
    spread = []
    for which, part in enumerate(coarse):
        scratch[which, pl.ds(0, rows // 2, stride=2), :] = part
        scratch[which, pl.ds(1, rows // 2, stride=2), :] = part
        spread.append(scratch[which, pl.ds(0, rows), :])
    top = jnp.maximum(fine[0], spread[0])
    here = jnp.exp2((fine[0] - top) * RATE) * float(1 << height)
    there = jnp.exp2((spread[0] - top) * RATE)
    return (top, here * fine[1] + there * spread[1], here * fine[2] + there * spread[2])


def bias_row(pieces):
    total = sum(count for count, _ in pieces)
    lane = lax.broadcasted_iota(jnp.int32, (1, total), 1)
    row = jnp.zeros((1, total), F32)
    start = 0
    for count, allowed in pieces:
        if allowed is not None:
            inside = (lane >= start) & (lane < start + count)
            row = jnp.where(inside, jnp.where(allowed, 0.0, MASKED), row)
        start += count
    return row


def edge_flags(height, position, ctx_size):
    span = max(1, (1 << height) // 4)
    block = position // span
    return block >= 1, block + 1 < ctx_size // span


def head_windows(position, ctx_size, halving, q, kv, left, right, thirds, fourths):
    everything = jnp.concatenate([kv, q], axis=1)
    levels = [everything]
    for _ in range(4):
        levels.append(pool(levels[-1], halving))
    q_at = [level[:, 2 * HEAD_DIM :] for level in levels]
    kv_at = [level[:, : 2 * HEAD_DIM] for level in levels]

    left0, right0 = left[0:128], right[0:128]
    left1 = jnp.concatenate([left[128:192], pool(left0, halving)], axis=0)
    right1 = jnp.concatenate([pool(right0, halving), right[128:192]], axis=0)
    left2 = jnp.concatenate([left[192:256], pool(left1, halving)], axis=0)
    right2 = jnp.concatenate([pool(right1, halving), right[192:256]], axis=0)

    def window(queries, pieces):
        rows = jnp.concatenate([piece for piece, _ in pieces], axis=0)
        bias = None
        if any(allowed is not None for _, allowed in pieces):
            bias = bias_row([(piece.shape[0], allowed) for piece, allowed in pieces])
        return queries, rows[:, :HEAD_DIM], rows[:, HEAD_DIM:], bias

    def halves(queries, before, has_before, after, has_after):
        return [
            window(queries[:HALF], [(before[:HALF], has_before), (after, has_after)]),
            window(queries[HALF:], [(before, has_before), (after[HALF:], has_after)]),
        ]

    has_left, has_right = edge_flags(4, position, ctx_size)
    is_right = position % 4 < 2
    mixed = (is_right & has_right) | (~is_right & has_left)
    pieces = []
    for chunks in (fourths[:3], fourths[3:]):
        pieces += list(zip(chunks, (has_left, has_right, mixed)))
    windows = [window(q_at[4], pieces)]

    has_left, has_right = edge_flags(3, position, ctx_size)
    odd = position % 2 == 1
    own = (odd & has_right) | (~odd & has_left)
    other = (odd & has_left) | (~odd & has_right)
    windows.append(window(q_at[3], [(thirds[0], own), (thirds[1], other), (thirds[2], other)]))

    has_left, has_right = edge_flags(2, position, ctx_size)
    windows += halves(q_at[2], left2, has_left, right2, has_right)

    kv1 = kv_at[1]
    windows += halves(q_at[1][:128], left1, has_left, kv1[128:], None)
    windows += halves(q_at[1][128:], kv1[:128], None, right1, has_right)

    windows.append(window(q[0:128], [(left0, has_left), (kv[0:256], None)]))
    for block in (1, 2):
        start = 128 * block
        windows.append(window(q[start : start + 128], [(kv[start - 128 : start + 256], None)]))
    windows.append(window(q[384:512], [(kv[256:512], None), (right0, has_right)]))
    return windows


def merge_windows(terms, scratch):
    peak, total, weight = terms[0]
    state = (peak, total * 16.0, weight * 16.0)
    for height, cut in ((3, slice(1, 2)), (2, slice(2, 4)), (1, slice(4, 8)), (0, slice(8, 12))):
        state = merged(height, stack(terms[cut]), state, scratch)
    return (state[1] / state[2]).astype(BF16)


SLOT_OFFSETS = [
    (-1, -1, -1, -1),
    (1, 1, 1, 1),
    (-2, 2, -2, 2),
    (-4, -4, -4, -4),
    (4, 4, 4, 4),
    (6, 6, -6, -6),
]
PASSED = 5
REACH = 7
CHUNKS = 8
AHEAD = 3
CHUNK_HEADS = HEADS // CHUNKS


def by_turn(turn, table):
    value = table[3]
    for at in (2, 1, 0):
        value = jnp.where(turn == at, table[at], value)
    return value


def inverse(table):
    back = [0, 0, 0, 0]
    for turn, offset in enumerate(table):
        back[(turn + offset) % 4] = -offset
    return tuple(back)


def layer_kernel(ctx_size, with_weight, *refs):
    if with_weight:
        q_ref, k_ref, v_ref, w_ref, out_ref = refs[:5]
        refs = refs[5:]
        w_all, w_recv, w_send, w_core = refs[-4:]
    else:
        q_ref, k_ref, v_ref, out_ref = refs[:4]
        refs = refs[4:]
    (to_right, to_left, third, fourth, rims, thirds, fourths, pooled, their_thirds,
     their_pooled, their_fourths, scratch, att, halving, send_sem, recv_sem,
     pass_send, pass_recv) = refs[:18]

    halving[...] = pooling_matrix()
    position = lax.axis_index("ctx")
    group = lax.axis_index("groups")
    turn = position % 4

    barrier = pltpu.get_barrier_semaphore()
    reach = ctx_size - 1 if with_weight else min(REACH, ctx_size - 1)
    for distance in range(1, reach + 1):
        for offset in (-distance, distance):
            peer = position + offset

            @pl.when((peer >= 0) & (peer < ctx_size))
            def _():
                pl.semaphore_signal(
                    barrier, inc=1, device_id={"ctx": peer}, device_id_type=pl.DeviceIdType.MESH
                )

    peers = jnp.minimum(position, reach) + jnp.minimum(ctx_size - 1 - position, reach)
    if with_weight:
        pl.semaphore_signal(
            barrier, inc=1, device_id={"groups": 1 - group}, device_id_type=pl.DeviceIdType.MESH
        )
        peers = peers + 1

    slots = [rims.at[0], rims.at[1], thirds] + [fourths.at[i] for i in range(3)]
    sources = [to_right, to_left, third] + [fourth] * 3
    passed = [thirds, pooled] + [fourths.at[i] for i in range(3)]
    passed_to = [their_thirds, their_pooled] + [their_fourths.at[i] for i in range(3)]
    sibling = position + 1 - 2 * (position % 2)
    givers = [position + by_turn(turn, table) for table in SLOT_OFFSETS]
    takers = [position + by_turn(turn, inverse(table)) for table in SLOT_OFFSETS]
    inside = lambda peer: (peer >= 0) & (peer < ctx_size)

    own_there = [inside(giver) for giver in givers]
    across = inside(position + 2 - 4 * (position % 2))
    send_there = [own_there[2], own_there[2]] + own_there[3:]
    pass_there = [across, across] + own_there[3:]

    pl.semaphore_wait(barrier, peers)

    for slot, there in zip(slots + passed_to, own_there + pass_there):

        @pl.when(jnp.logical_not(there))
        def _():
            slot[...] = jnp.zeros(slot.shape, BF16)

    def when(condition, action):
        if condition is None:
            action()
        else:
            pl.when(condition)(action)

    def slot_copy(chunk, which):
        heads = pl.ds(chunk * CHUNK_HEADS, CHUNK_HEADS)
        return pltpu.make_async_remote_copy(
            src_ref=sources[which].at[heads],
            dst_ref=slots[which].at[heads],
            send_sem=send_sem.at[chunk, which],
            recv_sem=recv_sem.at[chunk, which],
            device_id={"ctx": takers[which]},
            device_id_type=pl.DeviceIdType.MESH,
        )

    def pass_copy(chunk, which):
        heads = pl.ds(chunk * CHUNK_HEADS, CHUNK_HEADS)
        return pltpu.make_async_remote_copy(
            src_ref=passed[which].at[heads],
            dst_ref=passed_to[which].at[heads],
            send_sem=pass_send.at[chunk, which],
            recv_sem=pass_recv.at[chunk, which],
            device_id={"ctx": sibling},
            device_id_type=pl.DeviceIdType.MESH,
        )

    def forward(chunk):
        for which, there in enumerate(own_there):
            when(there, lambda which=which: slot_copy(chunk, which).wait_recv())
        lanes = []
        for at in range(CHUNK_HEADS):
            for which in range(2):
                lanes.append(rims[position % 2, chunk * CHUNK_HEADS + at, which])
        rows = jnp.concatenate(lanes, axis=1)
        eighth = jnp.concatenate(
            [
                pool(rows[192:256], halving),
                pool(pool(rows[128:192], halving), halving),
                pool(pool(pool(rows[0:128], halving), halving), halving),
            ],
            axis=0,
        )
        for at in range(CHUNK_HEADS):
            for which in range(2):
                start = (2 * at + which) * HEAD_DIM
                pooled[chunk * CHUNK_HEADS + at, which] = eighth[:, start : start + HEAD_DIM]
        for which, there in enumerate(send_there):
            when(there, lambda which=which: pass_copy(chunk, which).start())

    steps = []
    if with_weight:
        z = position // 4
        depth = ctx_size // 4
        partner = position + 2 - 4 * ((position // 2) % 2)

        def piece(shard, half, send, device):
            return pltpu.make_async_remote_copy(
                src_ref=w_all.at[shard, half],
                dst_ref=w_all.at[shard, half],
                send_sem=send,
                recv_sem=w_recv.at[shard, half],
                device_id=device,
                device_id_type=pl.DeviceIdType.MESH,
            )

        def to_x(shard):
            return piece(shard, group, w_send.at[0, shard], {"ctx": partner})

        def to_z(shard, way):
            kind = 1 if way > 0 else 2
            return piece(shard, group, w_send.at[kind, shard], {"ctx": position + 4 * way})

        def to_y(shard):
            return piece(shard, group, w_send.at[3, shard], {"groups": 1 - group})

        def to_core(shard, half, own):
            send = w_send.at[4, shard] if own else w_core.at[shard]
            return piece(shard, half, send, {"ctx": sibling})

        always = None
        can_go = {1: z + 1 < depth, -1: z >= 1}
        first = [(always, lambda: to_x(position))]
        for way in (1, -1):
            first.append((can_go[way], functools.partial(to_z, position, way)))
        first.append((always, lambda: to_core(position, group, True)))
        first.append((always, lambda: to_core(position, 1 - group, False)))
        steps.append([(always, None, first)])
        second = [(can_go[way], functools.partial(to_z, partner, way)) for way in (1, -1)]
        second.append((always, lambda: to_y(partner)))
        second.append((always, lambda: to_core(partner, group, True)))
        steps.append([(always, (partner, group), second)])
        for hops in range(1, depth):
            step = []
            for way in (1, -1):
                here = (z - hops * way >= 0) & (z - hops * way < depth)
                for base in (position, partner):
                    shard = base - 4 * hops * way
                    sends = [
                        (can_go[way], functools.partial(to_z, shard, way)),
                        (always, functools.partial(to_y, shard)),
                        (always, functools.partial(to_core, shard, group, True)),
                    ]
                    step.append((here, (shard, group), sends))
            steps.append(step)
        step = []
        for turns in range(depth):
            for base in (position, partner):
                if turns == 0 and base is position:
                    continue
                level = lax.rem(z + turns, depth)
                shard = base + 4 * (level - z)
                sends = [(always, functools.partial(to_core, shard, 1 - group, False))]
                step.append((always, (shard, 1 - group), sends))
        steps.append(step)

    def run_step(step):
        for here, awaited, sends in step:

            def act(awaited=awaited, sends=sends):
                if awaited is not None:
                    piece(*awaited, w_core.at[0], {"ctx": sibling}).wait_recv()
                for condition, copy in sends:
                    when(condition, lambda copy=copy: copy().start())

            when(here, act)

    def finish_step(step):
        for here, _, sends in step:

            def act(sends=sends):
                for condition, copy in sends:
                    when(condition, lambda copy=copy: copy().wait_send())

            when(here, act)

    if with_weight:
        w_all[position, 0] = w_ref[0:1024]
        w_all[position, 1] = w_ref[1024:2048]
        run_step(steps[0])

    def prepare(chunk, _):
        cols = CHUNK_HEADS * HEAD_DIM
        lanes = pl.ds(pl.multiple_of(chunk * cols, cols), cols)
        for which, ref in enumerate((k_ref, v_ref)):
            rows = ref[:, lanes]
            first = pool(rows, halving)
            second = pool(first, halving)
            eighth = pool(second, halving)
            sixteenth = pool(eighth, halving)
            for at in range(CHUNK_HEADS):
                head = chunk * CHUNK_HEADS + at
                cut = slice(at * HEAD_DIM, (at + 1) * HEAD_DIM)
                to_right[head, which, 0:128] = rows[384:512, cut]
                to_right[head, which, 128:192] = first[128:192, cut]
                to_right[head, which, 192:256] = second[0:64, cut]
                to_left[head, which, 0:128] = rows[0:128, cut]
                to_left[head, which, 128:192] = first[64:128, cut]
                to_left[head, which, 192:256] = second[64:128, cut]
                third[head, which] = eighth[:, cut]
                fourth[head, which] = sixteenth[:, cut]
        for which, taker in enumerate(takers):
            when(inside(taker), lambda which=which: slot_copy(chunk, which).start())
        return 0

    lax.fori_loop(0, AHEAD, prepare, 0)
    if with_weight:
        run_step(steps[1])
    forward(0)

    def one_chunk(chunk, _):
        @pl.when(chunk + AHEAD < CHUNKS)
        def _():
            prepare(chunk + AHEAD, 0)

        @pl.when(chunk + 1 < CHUNKS)
        def _():
            forward(chunk + 1)

        for which, there in enumerate(pass_there):
            when(there, lambda which=which: pass_copy(chunk, which).wait_recv())

        if with_weight:
            for at, step in enumerate(steps[2:]):
                pl.when(chunk == (1, 2, 4, 6)[at])(functools.partial(run_step, step))
        windows = []
        for at in range(CHUNK_HEADS):
            head = chunk * CHUNK_HEADS + at
            lanes = pl.ds(pl.multiple_of(head * HEAD_DIM, HEAD_DIM), HEAD_DIM)
            pair = lambda ref: jnp.concatenate([ref[head, 0], ref[head, 1]], axis=1)
            windows.append(
                head_windows(
                    position,
                    ctx_size,
                    halving,
                    q_ref[:, lanes],
                    jnp.concatenate([k_ref[:, lanes], v_ref[:, lanes]], axis=1),
                    pair(rims.at[0]),
                    pair(rims.at[1]),
                    [pair(ref) for ref in (thirds, their_thirds, their_pooled)],
                    [pair(ref.at[i]) for ref in (fourths, their_fourths) for i in range(3)],
                )
            )
        count = len(windows[0])
        terms = attend_all([one[at] for at in range(count) for one in windows])
        for at in range(CHUNK_HEADS):
            head = chunk * CHUNK_HEADS + at
            lanes = pl.ds(pl.multiple_of(head * HEAD_DIM, HEAD_DIM), HEAD_DIM)
            att[:, lanes] = merge_windows(terms[at::CHUNK_HEADS], scratch.at[at])
        return 0

    lax.fori_loop(0, CHUNKS, one_chunk, 0)

    if with_weight:
        for level in range(depth):
            for other in (0, 2):
                for half in range(2):
                    shard = 4 * level + other + 1 - position % 2
                    piece(shard, half, w_core.at[0], {"ctx": sibling}).wait_recv()

        def project(at, _):
            count = 2048
            weight = jnp.concatenate(
                [w_all[2 * at].reshape(count, 128), w_all[2 * at + 1].reshape(count, 128)], axis=1
            )
            result = jnp.dot(att[...], weight, preferred_element_type=F32)
            out_ref[:, pl.ds(pl.multiple_of(at * 256, 256), 256)] = result.astype(BF16)
            return 0

        lax.fori_loop(0, ctx_size // 2, project, 0)
        for step in steps:
            finish_step(step)
    else:
        out_ref[...] = att[...]

    def settle(chunk, _):
        for which, taker in enumerate(takers):
            when(inside(taker), lambda which=which: slot_copy(chunk, which).wait_send())
        for which, there in enumerate(send_there):
            when(there, lambda which=which: pass_copy(chunk, which).wait_send())
        return 0

    lax.fori_loop(0, CHUNKS, settle, 0)


def layer(ctx_size, queries, keys, values, weight=None):
    rows, width = queries.shape
    per_head = lambda *lead: pltpu.VMEM((*lead, HEAD_DIM), BF16)
    slots = len(SLOT_OFFSETS)
    scratch = [
        per_head(HEADS, 2, 256),
        per_head(HEADS, 2, 256),
        per_head(HEADS, 2, 64),
        per_head(HEADS, 2, 32),
        per_head(2, HEADS, 2, 256),
        per_head(HEADS, 2, 64),
        per_head(3, HEADS, 2, 32),
        per_head(HEADS, 2, 64),
        per_head(HEADS, 2, 64),
        per_head(HEADS, 2, 64),
        per_head(3, HEADS, 2, 32),
        pltpu.VMEM((CHUNK_HEADS, 3, rows, HEAD_DIM), F32),
        pltpu.VMEM((rows, width), BF16),
        pltpu.VMEM((BLOCK, 2 * BLOCK), BF16),
        pltpu.SemaphoreType.DMA((CHUNKS, slots)),
        pltpu.SemaphoreType.DMA((CHUNKS, slots)),
        pltpu.SemaphoreType.DMA((CHUNKS, PASSED)),
        pltpu.SemaphoreType.DMA((CHUNKS, PASSED)),
    ]
    operands = [queries, keys, values]
    if weight is not None:
        operands.append(weight)
        scratch += [
            pltpu.VMEM((ctx_size, 2, weight.shape[0] // 2, weight.shape[1]), BF16),
            pltpu.SemaphoreType.DMA((ctx_size, 2)),
            pltpu.SemaphoreType.DMA((5, ctx_size)),
            pltpu.SemaphoreType.DMA((ctx_size,)),
        ]
    return pl.pallas_call(
        functools.partial(layer_kernel, ctx_size, weight is not None),
        in_specs=[pl.BlockSpec(memory_space=pltpu.VMEM)] * len(operands),
        out_specs=pl.BlockSpec(memory_space=pltpu.VMEM),
        out_shape=jax.ShapeDtypeStruct((rows, width), BF16),
        scratch_shapes=scratch,
        compiler_params=pltpu.CompilerParams(
            collective_id=0, has_side_effects=True, vmem_limit_bytes=56 << 20
        ),
        name="layer",
    )(*operands)


def per_device(query_vectors, key_vectors, value_vectors, out_weight):
    ctx_size = lax.axis_size("ctx")
    in_kernel = (
        out_weight.shape[1] == 128 and ctx_size % 4 == 0 and lax.axis_size("groups") == 2
    )
    if in_kernel:
        return layer(ctx_size, query_vectors, key_vectors, value_vectors, out_weight)
    weight = lax.all_gather(out_weight, "ctx", axis=1, tiled=True)
    attended = layer(ctx_size, query_vectors, key_vectors, value_vectors)
    return jnp.dot(attended, weight, preferred_element_type=F32).astype(BF16)


def solution(mesh):
    in_specs = (
        P(("groups", "ctx"), None),
        P(("groups", "ctx"), None),
        P(("groups", "ctx"), None),
        P(None, "ctx"),
    )
    out_specs = P(("groups", "ctx"), None)
    return jax.shard_map(
        per_device, mesh=mesh, in_specs=in_specs, out_specs=out_specs, check_vma=False
    )
```

```python
import functools
import math

import jax
import jax.numpy as jnp
from jax import lax
from jax.experimental import pallas as pl
from jax.experimental.pallas import tpu as pltpu
from jax.sharding import PartitionSpec as P

HEADS = 16
HEAD_DIM = 128
BLOCK = 128
HALF = BLOCK // 2
BF16 = jnp.bfloat16
F32 = jnp.float32
RATE = HEAD_DIM ** (-0.5) * math.log2(math.e)
MASKED = -1e30


def pooling_matrix():
    at = lax.broadcasted_iota(jnp.int32, (BLOCK, 2 * BLOCK), 0)
    source = lax.broadcasted_iota(jnp.int32, (BLOCK, 2 * BLOCK), 1)
    return jnp.where((source >> 1) == at, 0.5, 0.0).astype(BF16)


def pool(rows, halving):
    means = []
    for start in range(0, rows.shape[0], 2 * BLOCK):
        part = rows[start : start + 2 * BLOCK]
        count = part.shape[0]
        half = halving[: count // 2, :count]
        means.append(jnp.dot(half, part, preferred_element_type=F32).astype(BF16))
    return means[0] if len(means) == 1 else jnp.concatenate(means, axis=0)


def raw_scores(queries, keys, _, bias):
    scores = lax.dot_general(queries, keys, (((1,), (1,)), ((), ())), preferred_element_type=F32)
    return scores if bias is None else scores + bias


def softmax_terms(scores, values):
    peak = jnp.max(scores, axis=1, keepdims=True)
    weights = jnp.exp2((scores - peak) * RATE).astype(BF16)
    ones = jnp.ones((values.shape[0], HEAD_DIM), BF16)
    both = jnp.dot(weights, jnp.concatenate([values, ones], axis=1), preferred_element_type=F32)
    return (
        jnp.broadcast_to(peak, (scores.shape[0], HEAD_DIM)),
        both[:, :HEAD_DIM],
        both[:, HEAD_DIM:],
    )


def attend_all(windows):
    ahead = 3
    scores, terms = {}, []
    for at in range(len(windows) + ahead):
        if at < len(windows):
            scores[at] = raw_scores(*windows[at])
        if at >= ahead:
            terms.append(softmax_terms(scores.pop(at - ahead), windows[at - ahead][2]))
    return terms


def stack(parts):
    return tuple(jnp.concatenate(items, axis=0) for items in zip(*parts))


def merged(height, fine, coarse, scratch):
    rows = fine[0].shape[0]
    spread = []
    for which, part in enumerate(coarse):
        scratch[which, pl.ds(0, rows // 2, stride=2), :] = part
        scratch[which, pl.ds(1, rows // 2, stride=2), :] = part
        spread.append(scratch[which, pl.ds(0, rows), :])
    top = jnp.maximum(fine[0], spread[0])
    here = jnp.exp2((fine[0] - top) * RATE) * float(1 << height)
    there = jnp.exp2((spread[0] - top) * RATE)
    return (top, here * fine[1] + there * spread[1], here * fine[2] + there * spread[2])


def bias_row(pieces):
    total = sum(count for count, _ in pieces)
    lane = lax.broadcasted_iota(jnp.int32, (1, total), 1)
    row = jnp.zeros((1, total), F32)
    start = 0
    for count, allowed in pieces:
        if allowed is not None:
            inside = (lane >= start) & (lane < start + count)
            row = jnp.where(inside, jnp.where(allowed, 0.0, MASKED), row)
        start += count
    return row


def edge_flags(height, position, ctx_size):
    span = max(1, (1 << height) // 4)
    block = position // span
    return block >= 1, block + 1 < ctx_size // span


def head_windows(position, ctx_size, halving, q, kv, left, right, thirds, fourths):
    everything = jnp.concatenate([kv, q], axis=1)
    levels = [everything]
    for _ in range(4):
        levels.append(pool(levels[-1], halving))
    q_at = [level[:, 2 * HEAD_DIM :] for level in levels]
    kv_at = [level[:, : 2 * HEAD_DIM] for level in levels]

    left0, right0 = left[0:128], right[0:128]
    left1 = jnp.concatenate([left[128:192], pool(left0, halving)], axis=0)
    right1 = jnp.concatenate([pool(right0, halving), right[128:192]], axis=0)
    left2 = jnp.concatenate([left[192:256], pool(left1, halving)], axis=0)
    right2 = jnp.concatenate([pool(right1, halving), right[192:256]], axis=0)

    def window(queries, pieces):
        rows = jnp.concatenate([piece for piece, _ in pieces], axis=0)
        bias = None
        if any(allowed is not None for _, allowed in pieces):
            bias = bias_row([(piece.shape[0], allowed) for piece, allowed in pieces])
        return queries, rows[:, :HEAD_DIM], rows[:, HEAD_DIM:], bias

    def halves(queries, before, has_before, after, has_after):
        return [
            window(queries[:HALF], [(before[:HALF], has_before), (after, has_after)]),
            window(queries[HALF:], [(before, has_before), (after[HALF:], has_after)]),
        ]

    has_left, has_right = edge_flags(4, position, ctx_size)
    is_right = position % 4 < 2
    mixed = (is_right & has_right) | (~is_right & has_left)
    pieces = []
    for chunks in (fourths[:3], fourths[3:]):
        pieces += list(zip(chunks, (has_left, has_right, mixed)))
    windows = [window(q_at[4], pieces)]

    has_left, has_right = edge_flags(3, position, ctx_size)
    odd = position % 2 == 1
    own = (odd & has_right) | (~odd & has_left)
    other = (odd & has_left) | (~odd & has_right)
    windows.append(window(q_at[3], [(thirds[0], own), (thirds[1], other), (thirds[2], other)]))

    has_left, has_right = edge_flags(2, position, ctx_size)
    windows += halves(q_at[2], left2, has_left, right2, has_right)

    kv1 = kv_at[1]
    windows += halves(q_at[1][:128], left1, has_left, kv1[128:], None)
    windows += halves(q_at[1][128:], kv1[:128], None, right1, has_right)

    windows.append(window(q[0:128], [(left0, has_left), (kv[0:256], None)]))
    for block in (1, 2):
        start = 128 * block
        windows.append(window(q[start : start + 128], [(kv[start - 128 : start + 256], None)]))
    windows.append(window(q[384:512], [(kv[256:512], None), (right0, has_right)]))
    return windows


def merge_windows(terms, scratch):
    peak, total, weight = terms[0]
    state = (peak, total * 16.0, weight * 16.0)
    for height, cut in ((3, slice(1, 2)), (2, slice(2, 4)), (1, slice(4, 8)), (0, slice(8, 12))):
        state = merged(height, stack(terms[cut]), state, scratch)
    return (state[1] / state[2]).astype(BF16)


SLOT_OFFSETS = [
    (-1, -1, -1, -1),
    (1, 1, 1, 1),
    (-2, 2, -2, 2),
    (-4, -4, -4, -4),
    (4, 4, 4, 4),
    (6, 6, -6, -6),
]
PASSED = 5
REACH = 7
CHUNKS = 8
AHEAD = 4
WEIGHT_CHUNKS = (0, 2, 4, 3, 3, 5, 7)
CHUNK_HEADS = HEADS // CHUNKS


def by_turn(turn, table):
    value = table[3]
    for at in (2, 1, 0):
        value = jnp.where(turn == at, table[at], value)
    return value


def inverse(table):
    back = [0, 0, 0, 0]
    for turn, offset in enumerate(table):
        back[(turn + offset) % 4] = -offset
    return tuple(back)


def layer_kernel(ctx_size, with_weight, *refs):
    if with_weight:
        q_ref, k_ref, v_ref, w_ref, out_ref = refs[:5]
        refs = refs[5:]
        w_all, w_recv, w_send, w_core = refs[-4:]
    else:
        q_ref, k_ref, v_ref, out_ref = refs[:4]
        refs = refs[4:]
    (to_right, to_left, third, fourth, rims, thirds, fourths, pooled, their_thirds,
     their_pooled, their_fourths, scratch, att, halving, send_sem, recv_sem,
     pass_send, pass_recv) = refs[:18]

    halving[...] = pooling_matrix()
    position = lax.axis_index("ctx")
    group = lax.axis_index("groups")
    turn = position % 4

    barrier = pltpu.get_barrier_semaphore()
    reach = ctx_size - 1 if with_weight else min(REACH, ctx_size - 1)
    for distance in range(1, reach + 1):
        for offset in (-distance, distance):
            peer = position + offset

            @pl.when((peer >= 0) & (peer < ctx_size))
            def _():
                pl.semaphore_signal(
                    barrier, inc=1, device_id={"ctx": peer}, device_id_type=pl.DeviceIdType.MESH
                )

    peers = jnp.minimum(position, reach) + jnp.minimum(ctx_size - 1 - position, reach)
    if with_weight:
        pl.semaphore_signal(
            barrier, inc=1, device_id={"groups": 1 - group}, device_id_type=pl.DeviceIdType.MESH
        )
        peers = peers + 1

    slots = [rims.at[0], rims.at[1], thirds] + [fourths.at[i] for i in range(3)]
    sources = [to_right, to_left, third] + [fourth] * 3
    passed = [thirds, pooled] + [fourths.at[i] for i in range(3)]
    passed_to = [their_thirds, their_pooled] + [their_fourths.at[i] for i in range(3)]
    sibling = position + 1 - 2 * (position % 2)
    givers = [position + by_turn(turn, table) for table in SLOT_OFFSETS]
    takers = [position + by_turn(turn, inverse(table)) for table in SLOT_OFFSETS]
    inside = lambda peer: (peer >= 0) & (peer < ctx_size)

    own_there = [inside(giver) for giver in givers]
    across = inside(position + 2 - 4 * (position % 2))
    send_there = [own_there[2], own_there[2]] + own_there[3:]
    pass_there = [across, across] + own_there[3:]

    pl.semaphore_wait(barrier, peers)

    for slot, there in zip(slots + passed_to, own_there + pass_there):

        @pl.when(jnp.logical_not(there))
        def _():
            slot[...] = jnp.zeros(slot.shape, BF16)

    def when(condition, action):
        if condition is None:
            action()
        else:
            pl.when(condition)(action)

    def slot_copy(chunk, which):
        heads = pl.ds(chunk * CHUNK_HEADS, CHUNK_HEADS)
        return pltpu.make_async_remote_copy(
            src_ref=sources[which].at[heads],
            dst_ref=slots[which].at[heads],
            send_sem=send_sem.at[chunk, which],
            recv_sem=recv_sem.at[chunk, which],
            device_id={"ctx": takers[which]},
            device_id_type=pl.DeviceIdType.MESH,
        )

    def pass_copy(chunk, which):
        heads = pl.ds(chunk * CHUNK_HEADS, CHUNK_HEADS)
        return pltpu.make_async_remote_copy(
            src_ref=passed[which].at[heads],
            dst_ref=passed_to[which].at[heads],
            send_sem=pass_send.at[chunk, which],
            recv_sem=pass_recv.at[chunk, which],
            device_id={"ctx": sibling},
            device_id_type=pl.DeviceIdType.MESH,
        )

    def forward(chunk):
        for which, there in enumerate(own_there):
            when(there, lambda which=which: slot_copy(chunk, which).wait_recv())
        lanes = []
        for at in range(CHUNK_HEADS):
            for which in range(2):
                lanes.append(rims[position % 2, chunk * CHUNK_HEADS + at, which])
        rows = jnp.concatenate(lanes, axis=1)
        eighth = jnp.concatenate(
            [
                pool(rows[192:256], halving),
                pool(pool(rows[128:192], halving), halving),
                pool(pool(pool(rows[0:128], halving), halving), halving),
            ],
            axis=0,
        )
        for at in range(CHUNK_HEADS):
            for which in range(2):
                start = (2 * at + which) * HEAD_DIM
                pooled[chunk * CHUNK_HEADS + at, which] = eighth[:, start : start + HEAD_DIM]
        for which, there in enumerate(send_there):
            when(there, lambda which=which: pass_copy(chunk, which).start())

    steps = []
    if with_weight:
        z = position // 4
        depth = ctx_size // 4
        partner = position + 2 - 4 * ((position // 2) % 2)

        def piece(shard, half, send, device):
            return pltpu.make_async_remote_copy(
                src_ref=w_all.at[shard, half],
                dst_ref=w_all.at[shard, half],
                send_sem=send,
                recv_sem=w_recv.at[shard, half],
                device_id=device,
                device_id_type=pl.DeviceIdType.MESH,
            )

        def to_x(shard):
            return piece(shard, group, w_send.at[0, shard], {"ctx": partner})

        def to_z(shard, way):
            kind = 1 if way > 0 else 2
            return piece(shard, group, w_send.at[kind, shard], {"ctx": position + 4 * way})

        def to_y(shard):
            return piece(shard, group, w_send.at[3, shard], {"groups": 1 - group})

        def to_core(shard, half, own):
            send = w_send.at[4, shard] if own else w_core.at[shard]
            return piece(shard, half, send, {"ctx": sibling})

        always = None
        can_go = {1: z + 1 < depth, -1: z >= 1}
        first = [(always, lambda: to_x(position))]
        for way in (1, -1):
            first.append((can_go[way], functools.partial(to_z, position, way)))
        first.append((always, lambda: to_core(position, group, True)))
        first.append((always, lambda: to_core(position, 1 - group, False)))
        steps.append([(always, None, first)])
        second = [(can_go[way], functools.partial(to_z, partner, way)) for way in (1, -1)]
        second.append((always, lambda: to_y(partner)))
        second.append((always, lambda: to_core(partner, group, True)))
        steps.append([(always, (partner, group), second)])
        for hops in range(1, depth):
            step = []
            for way in (1, -1):
                here = (z - hops * way >= 0) & (z - hops * way < depth)
                for base in (position, partner):
                    shard = base - 4 * hops * way
                    sends = [
                        (can_go[way], functools.partial(to_z, shard, way)),
                        (always, functools.partial(to_y, shard)),
                        (always, functools.partial(to_core, shard, group, True)),
                    ]
                    step.append((here, (shard, group), sends))
            steps.append(step)
        for hops in range(depth):
            step = []
            for way in (1, -1):
                here = (z - hops * way >= 0) & (z - hops * way < depth)
                for base in (position, partner):
                    if hops == 0 and (way < 0 or base is position):
                        continue
                    shard = base - 4 * hops * way
                    sends = [(always, functools.partial(to_core, shard, 1 - group, False))]
                    step.append((here, (shard, 1 - group), sends))
            steps.append(step)

    def run_step(step):
        for here, awaited, sends in step:

            def act(awaited=awaited, sends=sends):
                if awaited is not None:
                    piece(*awaited, w_core.at[0], {"ctx": sibling}).wait_recv()
                for condition, copy in sends:
                    when(condition, lambda copy=copy: copy().start())

            when(here, act)

    def finish_step(step):
        for here, _, sends in step:

            def act(sends=sends):
                for condition, copy in sends:
                    when(condition, lambda copy=copy: copy().wait_send())

            when(here, act)

    if with_weight:
        w_all[position, 0] = w_ref[0:1024]
        w_all[position, 1] = w_ref[1024:2048]
        run_step(steps[0])

    def prepare(chunk, _):
        cols = CHUNK_HEADS * HEAD_DIM
        lanes = pl.ds(pl.multiple_of(chunk * cols, cols), cols)
        for which, ref in enumerate((k_ref, v_ref)):
            rows = ref[:, lanes]
            first = pool(rows, halving)
            second = pool(first, halving)
            eighth = pool(second, halving)
            sixteenth = pool(eighth, halving)
            for at in range(CHUNK_HEADS):
                head = chunk * CHUNK_HEADS + at
                cut = slice(at * HEAD_DIM, (at + 1) * HEAD_DIM)
                to_right[head, which, 0:128] = rows[384:512, cut]
                to_right[head, which, 128:192] = first[128:192, cut]
                to_right[head, which, 192:256] = second[0:64, cut]
                to_left[head, which, 0:128] = rows[0:128, cut]
                to_left[head, which, 128:192] = first[64:128, cut]
                to_left[head, which, 192:256] = second[64:128, cut]
                third[head, which] = eighth[:, cut]
                fourth[head, which] = sixteenth[:, cut]
        for which, taker in enumerate(takers):
            when(inside(taker), lambda which=which: slot_copy(chunk, which).start())
        return 0

    lax.fori_loop(0, AHEAD, prepare, 0)
    if with_weight:
        run_step(steps[1])
    forward(0)

    def one_chunk(chunk, _):
        @pl.when(chunk + AHEAD < CHUNKS)
        def _():
            prepare(chunk + AHEAD, 0)

        @pl.when(chunk + 1 < CHUNKS)
        def _():
            forward(chunk + 1)

        for which, there in enumerate(pass_there):
            when(there, lambda which=which: pass_copy(chunk, which).wait_recv())

        if with_weight:
            for at, step in enumerate(steps[2:]):
                pl.when(chunk == WEIGHT_CHUNKS[at])(functools.partial(run_step, step))
        windows = []
        for at in range(CHUNK_HEADS):
            head = chunk * CHUNK_HEADS + at
            lanes = pl.ds(pl.multiple_of(head * HEAD_DIM, HEAD_DIM), HEAD_DIM)
            pair = lambda ref: jnp.concatenate([ref[head, 0], ref[head, 1]], axis=1)
            windows.append(
                head_windows(
                    position,
                    ctx_size,
                    halving,
                    q_ref[:, lanes],
                    jnp.concatenate([k_ref[:, lanes], v_ref[:, lanes]], axis=1),
                    pair(rims.at[0]),
                    pair(rims.at[1]),
                    [pair(ref) for ref in (thirds, their_thirds, their_pooled)],
                    [pair(ref.at[i]) for ref in (fourths, their_fourths) for i in range(3)],
                )
            )
        count = len(windows[0])
        terms = attend_all([one[at] for at in range(count) for one in windows])
        for at in range(CHUNK_HEADS):
            head = chunk * CHUNK_HEADS + at
            lanes = pl.ds(pl.multiple_of(head * HEAD_DIM, HEAD_DIM), HEAD_DIM)
            att[:, lanes] = merge_windows(terms[at::CHUNK_HEADS], scratch.at[at])
        return 0

    lax.fori_loop(0, CHUNKS, one_chunk, 0)

    if with_weight:
        def project(at, _):
            for half in range(2):
                theirs = 2 * at + 1 - position % 2
                piece(theirs, half, w_core.at[0], {"ctx": sibling}).wait_recv()
            count = 2048
            weight = jnp.concatenate(
                [w_all[2 * at].reshape(count, 128), w_all[2 * at + 1].reshape(count, 128)], axis=1
            )
            result = jnp.dot(att[...], weight, preferred_element_type=F32)
            out_ref[:, pl.ds(pl.multiple_of(at * 256, 256), 256)] = result.astype(BF16)
            return 0

        lax.fori_loop(0, ctx_size // 2, project, 0)
        for step in steps:
            finish_step(step)
    else:
        out_ref[...] = att[...]

    def settle(chunk, _):
        for which, taker in enumerate(takers):
            when(inside(taker), lambda which=which: slot_copy(chunk, which).wait_send())
        for which, there in enumerate(send_there):
            when(there, lambda which=which: pass_copy(chunk, which).wait_send())
        return 0

    lax.fori_loop(0, CHUNKS, settle, 0)


def layer(ctx_size, queries, keys, values, weight=None):
    rows, width = queries.shape
    per_head = lambda *lead: pltpu.VMEM((*lead, HEAD_DIM), BF16)
    slots = len(SLOT_OFFSETS)
    scratch = [
        per_head(HEADS, 2, 256),
        per_head(HEADS, 2, 256),
        per_head(HEADS, 2, 64),
        per_head(HEADS, 2, 32),
        per_head(2, HEADS, 2, 256),
        per_head(HEADS, 2, 64),
        per_head(3, HEADS, 2, 32),
        per_head(HEADS, 2, 64),
        per_head(HEADS, 2, 64),
        per_head(HEADS, 2, 64),
        per_head(3, HEADS, 2, 32),
        pltpu.VMEM((CHUNK_HEADS, 3, rows, HEAD_DIM), F32),
        pltpu.VMEM((rows, width), BF16),
        pltpu.VMEM((BLOCK, 2 * BLOCK), BF16),
        pltpu.SemaphoreType.DMA((CHUNKS, slots)),
        pltpu.SemaphoreType.DMA((CHUNKS, slots)),
        pltpu.SemaphoreType.DMA((CHUNKS, PASSED)),
        pltpu.SemaphoreType.DMA((CHUNKS, PASSED)),
    ]
    operands = [queries, keys, values]
    if weight is not None:
        operands.append(weight)
        scratch += [
            pltpu.VMEM((ctx_size, 2, weight.shape[0] // 2, weight.shape[1]), BF16),
            pltpu.SemaphoreType.DMA((ctx_size, 2)),
            pltpu.SemaphoreType.DMA((5, ctx_size)),
            pltpu.SemaphoreType.DMA((ctx_size,)),
        ]
    return pl.pallas_call(
        functools.partial(layer_kernel, ctx_size, weight is not None),
        in_specs=[pl.BlockSpec(memory_space=pltpu.VMEM)] * len(operands),
        out_specs=pl.BlockSpec(memory_space=pltpu.VMEM),
        out_shape=jax.ShapeDtypeStruct((rows, width), BF16),
        scratch_shapes=scratch,
        compiler_params=pltpu.CompilerParams(
            collective_id=0, has_side_effects=True, vmem_limit_bytes=56 << 20
        ),
        name="layer",
    )(*operands)


def per_device(query_vectors, key_vectors, value_vectors, out_weight):
    ctx_size = lax.axis_size("ctx")
    in_kernel = (
        out_weight.shape[1] == 128 and ctx_size == 16 and lax.axis_size("groups") == 2
    )
    if in_kernel:
        return layer(ctx_size, query_vectors, key_vectors, value_vectors, out_weight)
    weight = lax.all_gather(out_weight, "ctx", axis=1, tiled=True)
    attended = layer(ctx_size, query_vectors, key_vectors, value_vectors)
    return jnp.dot(attended, weight, preferred_element_type=F32).astype(BF16)


def solution(mesh):
    in_specs = (
        P(("groups", "ctx"), None),
        P(("groups", "ctx"), None),
        P(("groups", "ctx"), None),
        P(None, "ctx"),
    )
    out_specs = P(("groups", "ctx"), None)
    return jax.shard_map(
        per_device, mesh=mesh, in_specs=in_specs, out_specs=out_specs, check_vma=False
    )
```

```python
import functools
import math

import jax
import jax.numpy as jnp
from jax import lax
from jax.experimental import pallas as pl
from jax.experimental.pallas import tpu as pltpu
from jax.sharding import PartitionSpec as P

HEADS = 16
HEAD_DIM = 128
BLOCK = 128
HALF = BLOCK // 2
BF16 = jnp.bfloat16
F32 = jnp.float32
RATE = HEAD_DIM ** (-0.5) * math.log2(math.e)
MASKED = -1e30


def pooling_matrix():
    at = lax.broadcasted_iota(jnp.int32, (BLOCK, 2 * BLOCK), 0)
    source = lax.broadcasted_iota(jnp.int32, (BLOCK, 2 * BLOCK), 1)
    return jnp.where((source >> 1) == at, 0.5, 0.0).astype(BF16)


def pool(rows, halving):
    means = []
    for start in range(0, rows.shape[0], 2 * BLOCK):
        part = rows[start : start + 2 * BLOCK]
        count = part.shape[0]
        half = halving[: count // 2, :count]
        means.append(jnp.dot(half, part, preferred_element_type=F32).astype(BF16))
    return means[0] if len(means) == 1 else jnp.concatenate(means, axis=0)


def admission_bias():
    row = lax.broadcasted_iota(jnp.int32, (BLOCK, 2 * BLOCK), 0)
    key = lax.broadcasted_iota(jnp.int32, (BLOCK, 2 * BLOCK), 1)
    upper = row >= HALF
    left_ok = (key < BLOCK) & (upper | (key < HALF))
    right_ok = (key >= BLOCK) & (jnp.logical_not(upper) | (key >= BLOCK + HALF))
    return jnp.where(left_ok | right_ok, 0.0, MASKED)


def raw_scores(queries, keys, _, biases):
    scores = lax.dot_general(queries, keys, (((1,), (1,)), ((), ())), preferred_element_type=F32)
    if len(biases) == 1:
        parts = [scores]
    else:
        parts = [scores[:BLOCK, : 3 * BLOCK], scores[BLOCK:, BLOCK:]]
    return [part if bias is None else part + bias for part, bias in zip(parts, biases)]


def softmax_terms(parts, values):
    peaks, weights = [], []
    for scores in parts:
        peak = jnp.max(scores, axis=1, keepdims=True)
        weights.append(jnp.exp2((scores - peak) * RATE).astype(BF16))
        peaks.append(jnp.broadcast_to(peak, (scores.shape[0], HEAD_DIM)))
    if len(parts) == 2:
        none = jnp.zeros((BLOCK, BLOCK), BF16)
        weights = [
            jnp.concatenate([weights[0], none], axis=1),
            jnp.concatenate([none, weights[1]], axis=1),
        ]
    weights = jnp.concatenate(weights, axis=0) if len(weights) == 2 else weights[0]
    peak = jnp.concatenate(peaks, axis=0) if len(peaks) == 2 else peaks[0]
    ones = jnp.ones((values.shape[0], HEAD_DIM), BF16)
    both = jnp.dot(weights, jnp.concatenate([values, ones], axis=1), preferred_element_type=F32)
    return peak, both[:, :HEAD_DIM], both[:, HEAD_DIM:]


def attend_all(windows):
    ahead = 2
    scores, terms = {}, []
    for at in range(len(windows) + ahead):
        if at < len(windows):
            scores[at] = raw_scores(*windows[at])
        if at >= ahead:
            terms.append(softmax_terms(scores.pop(at - ahead), windows[at - ahead][2]))
    return terms


def stack(parts):
    return tuple(jnp.concatenate(items, axis=0) for items in zip(*parts))


def merged(height, fine, coarse, scratch):
    rows = fine[0].shape[0]
    spread = []
    for which, part in enumerate(coarse):
        scratch[which, pl.ds(0, rows // 2, stride=2), :] = part
        scratch[which, pl.ds(1, rows // 2, stride=2), :] = part
        spread.append(scratch[which, pl.ds(0, rows), :])
    top = jnp.maximum(fine[0], spread[0])
    here = jnp.exp2((fine[0] - top) * RATE) * float(1 << height)
    there = jnp.exp2((spread[0] - top) * RATE)
    return (top, here * fine[1] + there * spread[1], here * fine[2] + there * spread[2])


def bias_row(pieces):
    total = sum(count for count, _ in pieces)
    lane = lax.broadcasted_iota(jnp.int32, (1, total), 1)
    row = jnp.zeros((1, total), F32)
    start = 0
    for count, allowed in pieces:
        if allowed is not None:
            inside = (lane >= start) & (lane < start + count)
            row = jnp.where(inside, jnp.where(allowed, 0.0, MASKED), row)
        start += count
    return row


def edge_flags(height, position, ctx_size):
    span = max(1, (1 << height) // 4)
    block = position // span
    return block >= 1, block + 1 < ctx_size // span


def head_windows(position, ctx_size, halving, admission, q, kv, left, right, thirds, fourths):
    everything = jnp.concatenate([kv, q], axis=1)
    levels = [everything]
    for _ in range(4):
        levels.append(pool(levels[-1], halving))
    q_at = [level[:, 2 * HEAD_DIM :] for level in levels]
    kv_at = [level[:, : 2 * HEAD_DIM] for level in levels]

    left0, right0 = left[0:128], right[0:128]
    left1 = jnp.concatenate([left[128:192], pool(left0, halving)], axis=0)
    right1 = jnp.concatenate([pool(right0, halving), right[128:192]], axis=0)
    left2 = jnp.concatenate([left[192:256], pool(left1, halving)], axis=0)
    right2 = jnp.concatenate([pool(right1, halving), right[192:256]], axis=0)

    def window(queries, pieces, admitted=None):
        rows = jnp.concatenate([piece for piece, _ in pieces], axis=0)
        bias = admitted
        if any(allowed is not None for _, allowed in pieces):
            edge = bias_row([(piece.shape[0], allowed) for piece, allowed in pieces])
            bias = edge if admitted is None else admitted + edge
        return queries, rows[:, :HEAD_DIM], rows[:, HEAD_DIM:], (bias,)

    def two_blocks(queries, rows, biases):
        return queries, rows[:, :HEAD_DIM], rows[:, HEAD_DIM:], biases

    has_left, has_right = edge_flags(4, position, ctx_size)
    is_right = position % 4 < 2
    mixed = (is_right & has_right) | (~is_right & has_left)
    pieces = []
    for chunks in (fourths[:3], fourths[3:]):
        pieces += list(zip(chunks, (has_left, has_right, mixed)))
    windows = [window(q_at[4], pieces)]

    has_left, has_right = edge_flags(3, position, ctx_size)
    odd = position % 2 == 1
    own = (odd & has_right) | (~odd & has_left)
    other = (odd & has_left) | (~odd & has_right)
    windows.append(window(q_at[3], [(thirds[0], own), (thirds[1], other), (thirds[2], other)]))

    has_left, has_right = edge_flags(2, position, ctx_size)
    windows.append(window(q_at[2], [(left2, has_left), (right2, has_right)], admission))

    q1, kv1 = q_at[1], kv_at[1]
    windows.append(window(q1[:128], [(left1, has_left), (kv1[128:], None)], admission))
    windows.append(window(q1[128:], [(kv1[:128], None), (right1, has_right)], admission))

    first = bias_row([(128, has_left), (256, None)])
    last = bias_row([(256, None), (128, has_right)])
    windows.append(two_blocks(q[:256], jnp.concatenate([left0, kv[:384]], axis=0), (first, None)))
    windows.append(two_blocks(q[256:], jnp.concatenate([kv[128:], right0], axis=0), (None, last)))
    return windows


def merge_windows(terms, scratch):
    peak, total, weight = terms[0]
    state = (peak, total * 16.0, weight * 16.0)
    for height, cut in ((3, slice(1, 2)), (2, slice(2, 3)), (1, slice(3, 5)), (0, slice(5, 7))):
        state = merged(height, stack(terms[cut]), state, scratch)
    return (state[1] / state[2]).astype(BF16)


SLOT_OFFSETS = [
    (-1, -1, -1, -1),
    (1, 1, 1, 1),
    (-2, 2, -2, 2),
    (-4, -4, -4, -4),
    (4, 4, 4, 4),
    (6, 6, -6, -6),
]
PASSED = 5
REACH = 7
CHUNKS = 8
AHEAD = 4
WEIGHT_CHUNKS = (0, 2, 4, 3, 3, 5, 7)
CHUNK_HEADS = HEADS // CHUNKS


def by_turn(turn, table):
    value = table[3]
    for at in (2, 1, 0):
        value = jnp.where(turn == at, table[at], value)
    return value


def inverse(table):
    back = [0, 0, 0, 0]
    for turn, offset in enumerate(table):
        back[(turn + offset) % 4] = -offset
    return tuple(back)


def layer_kernel(ctx_size, with_weight, *refs):
    if with_weight:
        q_ref, k_ref, v_ref, w_ref, out_ref = refs[:5]
        refs = refs[5:]
        w_all, w_recv, w_send, w_core = refs[-4:]
    else:
        q_ref, k_ref, v_ref, out_ref = refs[:4]
        refs = refs[4:]
    (to_right, to_left, third, fourth, rims, thirds, fourths, pooled, their_thirds,
     their_pooled, their_fourths, scratch, att, halving, admission, send_sem,
     recv_sem, pass_send, pass_recv) = refs[:19]

    halving[...] = pooling_matrix()
    admission[...] = admission_bias()
    position = lax.axis_index("ctx")
    group = lax.axis_index("groups")
    turn = position % 4

    barrier = pltpu.get_barrier_semaphore()
    reach = ctx_size - 1 if with_weight else min(REACH, ctx_size - 1)
    for distance in range(1, reach + 1):
        for offset in (-distance, distance):
            peer = position + offset

            @pl.when((peer >= 0) & (peer < ctx_size))
            def _():
                pl.semaphore_signal(
                    barrier, inc=1, device_id={"ctx": peer}, device_id_type=pl.DeviceIdType.MESH
                )

    peers = jnp.minimum(position, reach) + jnp.minimum(ctx_size - 1 - position, reach)
    if with_weight:
        pl.semaphore_signal(
            barrier, inc=1, device_id={"groups": 1 - group}, device_id_type=pl.DeviceIdType.MESH
        )
        peers = peers + 1

    slots = [rims.at[0], rims.at[1], thirds] + [fourths.at[i] for i in range(3)]
    sources = [to_right, to_left, third] + [fourth] * 3
    passed = [thirds, pooled] + [fourths.at[i] for i in range(3)]
    passed_to = [their_thirds, their_pooled] + [their_fourths.at[i] for i in range(3)]
    sibling = position + 1 - 2 * (position % 2)
    givers = [position + by_turn(turn, table) for table in SLOT_OFFSETS]
    takers = [position + by_turn(turn, inverse(table)) for table in SLOT_OFFSETS]
    inside = lambda peer: (peer >= 0) & (peer < ctx_size)

    own_there = [inside(giver) for giver in givers]
    across = inside(position + 2 - 4 * (position % 2))
    send_there = [own_there[2], own_there[2]] + own_there[3:]
    pass_there = [across, across] + own_there[3:]

    pl.semaphore_wait(barrier, peers)

    for slot, there in zip(slots + passed_to, own_there + pass_there):

        @pl.when(jnp.logical_not(there))
        def _():
            slot[...] = jnp.zeros(slot.shape, BF16)

    def when(condition, action):
        if condition is None:
            action()
        else:
            pl.when(condition)(action)

    def slot_copy(chunk, which):
        heads = pl.ds(chunk * CHUNK_HEADS, CHUNK_HEADS)
        return pltpu.make_async_remote_copy(
            src_ref=sources[which].at[heads],
            dst_ref=slots[which].at[heads],
            send_sem=send_sem.at[chunk, which],
            recv_sem=recv_sem.at[chunk, which],
            device_id={"ctx": takers[which]},
            device_id_type=pl.DeviceIdType.MESH,
        )

    def pass_copy(chunk, which):
        heads = pl.ds(chunk * CHUNK_HEADS, CHUNK_HEADS)
        return pltpu.make_async_remote_copy(
            src_ref=passed[which].at[heads],
            dst_ref=passed_to[which].at[heads],
            send_sem=pass_send.at[chunk, which],
            recv_sem=pass_recv.at[chunk, which],
            device_id={"ctx": sibling},
            device_id_type=pl.DeviceIdType.MESH,
        )

    def forward(chunk):
        for which, there in enumerate(own_there):
            when(there, lambda which=which: slot_copy(chunk, which).wait_recv())
        lanes = []
        for at in range(CHUNK_HEADS):
            for which in range(2):
                lanes.append(rims[position % 2, chunk * CHUNK_HEADS + at, which])
        rows = jnp.concatenate(lanes, axis=1)
        eighth = jnp.concatenate(
            [
                pool(rows[192:256], halving),
                pool(pool(rows[128:192], halving), halving),
                pool(pool(pool(rows[0:128], halving), halving), halving),
            ],
            axis=0,
        )
        for at in range(CHUNK_HEADS):
            for which in range(2):
                start = (2 * at + which) * HEAD_DIM
                pooled[chunk * CHUNK_HEADS + at, which] = eighth[:, start : start + HEAD_DIM]
        for which, there in enumerate(send_there):
            when(there, lambda which=which: pass_copy(chunk, which).start())

    steps = []
    if with_weight:
        z = position // 4
        depth = ctx_size // 4
        partner = position + 2 - 4 * ((position // 2) % 2)

        def piece(shard, half, send, device):
            return pltpu.make_async_remote_copy(
                src_ref=w_all.at[shard, half],
                dst_ref=w_all.at[shard, half],
                send_sem=send,
                recv_sem=w_recv.at[shard, half],
                device_id=device,
                device_id_type=pl.DeviceIdType.MESH,
            )

        def to_x(shard):
            return piece(shard, group, w_send.at[0, shard], {"ctx": partner})

        def to_z(shard, way):
            kind = 1 if way > 0 else 2
            return piece(shard, group, w_send.at[kind, shard], {"ctx": position + 4 * way})

        def to_y(shard):
            return piece(shard, group, w_send.at[3, shard], {"groups": 1 - group})

        def to_core(shard, half, own):
            send = w_send.at[4, shard] if own else w_core.at[shard]
            return piece(shard, half, send, {"ctx": sibling})

        always = None
        can_go = {1: z + 1 < depth, -1: z >= 1}
        first = [(always, lambda: to_x(position))]
        for way in (1, -1):
            first.append((can_go[way], functools.partial(to_z, position, way)))
        first.append((always, lambda: to_core(position, group, True)))
        first.append((always, lambda: to_core(position, 1 - group, False)))
        steps.append([(always, None, first)])
        second = [(can_go[way], functools.partial(to_z, partner, way)) for way in (1, -1)]
        second.append((always, lambda: to_y(partner)))
        second.append((always, lambda: to_core(partner, group, True)))
        steps.append([(always, (partner, group), second)])
        for hops in range(1, depth):
            step = []
            for way in (1, -1):
                here = (z - hops * way >= 0) & (z - hops * way < depth)
                for base in (position, partner):
                    shard = base - 4 * hops * way
                    sends = [
                        (can_go[way], functools.partial(to_z, shard, way)),
                        (always, functools.partial(to_y, shard)),
                        (always, functools.partial(to_core, shard, group, True)),
                    ]
                    step.append((here, (shard, group), sends))
            steps.append(step)
        for hops in range(depth):
            step = []
            for way in (1, -1):
                here = (z - hops * way >= 0) & (z - hops * way < depth)
                for base in (position, partner):
                    if hops == 0 and (way < 0 or base is position):
                        continue
                    shard = base - 4 * hops * way
                    sends = [(always, functools.partial(to_core, shard, 1 - group, False))]
                    step.append((here, (shard, 1 - group), sends))
            steps.append(step)

    def run_step(step):
        for here, awaited, sends in step:

            def act(awaited=awaited, sends=sends):
                if awaited is not None:
                    piece(*awaited, w_core.at[0], {"ctx": sibling}).wait_recv()
                for condition, copy in sends:
                    when(condition, lambda copy=copy: copy().start())

            when(here, act)

    def finish_step(step):
        for here, _, sends in step:

            def act(sends=sends):
                for condition, copy in sends:
                    when(condition, lambda copy=copy: copy().wait_send())

            when(here, act)

    if with_weight:
        w_all[position, 0] = w_ref[0:1024]
        w_all[position, 1] = w_ref[1024:2048]
        run_step(steps[0])

    def prepare(chunk, _):
        cols = CHUNK_HEADS * HEAD_DIM
        lanes = pl.ds(pl.multiple_of(chunk * cols, cols), cols)
        for which, ref in enumerate((k_ref, v_ref)):
            rows = ref[:, lanes]
            first = pool(rows, halving)
            second = pool(first, halving)
            eighth = pool(second, halving)
            sixteenth = pool(eighth, halving)
            for at in range(CHUNK_HEADS):
                head = chunk * CHUNK_HEADS + at
                cut = slice(at * HEAD_DIM, (at + 1) * HEAD_DIM)
                to_right[head, which, 0:128] = rows[384:512, cut]
                to_right[head, which, 128:192] = first[128:192, cut]
                to_right[head, which, 192:256] = second[0:64, cut]
                to_left[head, which, 0:128] = rows[0:128, cut]
                to_left[head, which, 128:192] = first[64:128, cut]
                to_left[head, which, 192:256] = second[64:128, cut]
                third[head, which] = eighth[:, cut]
                fourth[head, which] = sixteenth[:, cut]
        for which, taker in enumerate(takers):
            when(inside(taker), lambda which=which: slot_copy(chunk, which).start())
        return 0

    lax.fori_loop(0, AHEAD, prepare, 0)
    if with_weight:
        run_step(steps[1])
    forward(0)

    def one_chunk(chunk, _):
        @pl.when(chunk + AHEAD < CHUNKS)
        def _():
            prepare(chunk + AHEAD, 0)

        @pl.when(chunk + 1 < CHUNKS)
        def _():
            forward(chunk + 1)

        for which, there in enumerate(pass_there):
            when(there, lambda which=which: pass_copy(chunk, which).wait_recv())

        if with_weight:
            for at, step in enumerate(steps[2:]):
                pl.when(chunk == WEIGHT_CHUNKS[at])(functools.partial(run_step, step))
        windows = []
        for at in range(CHUNK_HEADS):
            head = chunk * CHUNK_HEADS + at
            lanes = pl.ds(pl.multiple_of(head * HEAD_DIM, HEAD_DIM), HEAD_DIM)
            pair = lambda ref: jnp.concatenate([ref[head, 0], ref[head, 1]], axis=1)
            windows.append(
                head_windows(
                    position,
                    ctx_size,
                    halving,
                    admission[...],
                    q_ref[:, lanes],
                    jnp.concatenate([k_ref[:, lanes], v_ref[:, lanes]], axis=1),
                    pair(rims.at[0]),
                    pair(rims.at[1]),
                    [pair(ref) for ref in (thirds, their_thirds, their_pooled)],
                    [pair(ref.at[i]) for ref in (fourths, their_fourths) for i in range(3)],
                )
            )
        count = len(windows[0])
        terms = attend_all([one[at] for at in range(count) for one in windows])
        for at in range(CHUNK_HEADS):
            head = chunk * CHUNK_HEADS + at
            lanes = pl.ds(pl.multiple_of(head * HEAD_DIM, HEAD_DIM), HEAD_DIM)
            att[:, lanes] = merge_windows(terms[at::CHUNK_HEADS], scratch.at[at])
        return 0

    lax.fori_loop(0, CHUNKS, one_chunk, 0)

    if with_weight:
        def project(at, _):
            for half in range(2):
                theirs = 2 * at + 1 - position % 2
                piece(theirs, half, w_core.at[0], {"ctx": sibling}).wait_recv()
            count = 2048
            weight = jnp.concatenate(
                [w_all[2 * at].reshape(count, 128), w_all[2 * at + 1].reshape(count, 128)], axis=1
            )
            result = jnp.dot(att[...], weight, preferred_element_type=F32)
            out_ref[:, pl.ds(pl.multiple_of(at * 256, 256), 256)] = result.astype(BF16)
            return 0

        lax.fori_loop(0, ctx_size // 2, project, 0)
        for step in steps:
            finish_step(step)
    else:
        out_ref[...] = att[...]

    def settle(chunk, _):
        for which, taker in enumerate(takers):
            when(inside(taker), lambda which=which: slot_copy(chunk, which).wait_send())
        for which, there in enumerate(send_there):
            when(there, lambda which=which: pass_copy(chunk, which).wait_send())
        return 0

    lax.fori_loop(0, CHUNKS, settle, 0)


def layer(ctx_size, queries, keys, values, weight=None):
    rows, width = queries.shape
    per_head = lambda *lead: pltpu.VMEM((*lead, HEAD_DIM), BF16)
    slots = len(SLOT_OFFSETS)
    scratch = [
        per_head(HEADS, 2, 256),
        per_head(HEADS, 2, 256),
        per_head(HEADS, 2, 64),
        per_head(HEADS, 2, 32),
        per_head(2, HEADS, 2, 256),
        per_head(HEADS, 2, 64),
        per_head(3, HEADS, 2, 32),
        per_head(HEADS, 2, 64),
        per_head(HEADS, 2, 64),
        per_head(HEADS, 2, 64),
        per_head(3, HEADS, 2, 32),
        pltpu.VMEM((CHUNK_HEADS, 3, rows, HEAD_DIM), F32),
        pltpu.VMEM((rows, width), BF16),
        pltpu.VMEM((BLOCK, 2 * BLOCK), BF16),
        pltpu.VMEM((BLOCK, 2 * BLOCK), F32),
        pltpu.SemaphoreType.DMA((CHUNKS, slots)),
        pltpu.SemaphoreType.DMA((CHUNKS, slots)),
        pltpu.SemaphoreType.DMA((CHUNKS, PASSED)),
        pltpu.SemaphoreType.DMA((CHUNKS, PASSED)),
    ]
    operands = [queries, keys, values]
    if weight is not None:
        operands.append(weight)
        scratch += [
            pltpu.VMEM((ctx_size, 2, weight.shape[0] // 2, weight.shape[1]), BF16),
            pltpu.SemaphoreType.DMA((ctx_size, 2)),
            pltpu.SemaphoreType.DMA((5, ctx_size)),
            pltpu.SemaphoreType.DMA((ctx_size,)),
        ]
    return pl.pallas_call(
        functools.partial(layer_kernel, ctx_size, weight is not None),
        in_specs=[pl.BlockSpec(memory_space=pltpu.VMEM)] * len(operands),
        out_specs=pl.BlockSpec(memory_space=pltpu.VMEM),
        out_shape=jax.ShapeDtypeStruct((rows, width), BF16),
        scratch_shapes=scratch,
        compiler_params=pltpu.CompilerParams(
            collective_id=0, has_side_effects=True, vmem_limit_bytes=56 << 20
        ),
        name="layer",
    )(*operands)


def per_device(query_vectors, key_vectors, value_vectors, out_weight):
    ctx_size = lax.axis_size("ctx")
    in_kernel = (
        out_weight.shape[1] == 128 and ctx_size == 16 and lax.axis_size("groups") == 2
    )
    if in_kernel:
        return layer(ctx_size, query_vectors, key_vectors, value_vectors, out_weight)
    weight = lax.all_gather(out_weight, "ctx", axis=1, tiled=True)
    attended = layer(ctx_size, query_vectors, key_vectors, value_vectors)
    return jnp.dot(attended, weight, preferred_element_type=F32).astype(BF16)


def solution(mesh):
    in_specs = (
        P(("groups", "ctx"), None),
        P(("groups", "ctx"), None),
        P(("groups", "ctx"), None),
        P(None, "ctx"),
    )
    out_specs = P(("groups", "ctx"), None)
    return jax.shard_map(
        per_device, mesh=mesh, in_specs=in_specs, out_specs=out_specs, check_vma=False
    )
```

```python
import functools
import math

import jax
import jax.numpy as jnp
from jax import lax
from jax.experimental import pallas as pl
from jax.experimental.pallas import tpu as pltpu
from jax.sharding import PartitionSpec as P

HEADS = 16
HEAD_DIM = 128
BLOCK = 128
HALF = BLOCK // 2
BF16 = jnp.bfloat16
F32 = jnp.float32
RATE = HEAD_DIM ** (-0.5) * math.log2(math.e)
MASKED = -1e30


def pooling_matrix():
    at = lax.broadcasted_iota(jnp.int32, (BLOCK, 2 * BLOCK), 0)
    source = lax.broadcasted_iota(jnp.int32, (BLOCK, 2 * BLOCK), 1)
    return jnp.where((source >> 1) == at, 0.5, 0.0).astype(BF16)


def pool(rows, halving):
    means = []
    for start in range(0, rows.shape[0], 2 * BLOCK):
        part = rows[start : start + 2 * BLOCK]
        count = part.shape[0]
        half = halving[: count // 2, :count]
        means.append(jnp.dot(half, part, preferred_element_type=F32).astype(BF16))
    return means[0] if len(means) == 1 else jnp.concatenate(means, axis=0)


def admission_bias():
    row = lax.broadcasted_iota(jnp.int32, (BLOCK, 2 * BLOCK), 0)
    key = lax.broadcasted_iota(jnp.int32, (BLOCK, 2 * BLOCK), 1)
    upper = row >= HALF
    left_ok = (key < BLOCK) & (upper | (key < HALF))
    right_ok = (key >= BLOCK) & (jnp.logical_not(upper) | (key >= BLOCK + HALF))
    return jnp.where(left_ok | right_ok, 0.0, MASKED)


def raw_scores(queries, keys, _, biases):
    scores = lax.dot_general(queries, keys, (((1,), (1,)), ((), ())), preferred_element_type=F32)
    if len(biases) == 1:
        parts = [scores]
    else:
        parts = [scores[:BLOCK, : 3 * BLOCK], scores[BLOCK:, BLOCK:]]
    return [part if bias is None else part + bias for part, bias in zip(parts, biases)]


def softmax_terms(parts, values):
    peaks, weights = [], []
    for scores in parts:
        peak = jnp.max(scores, axis=1, keepdims=True)
        weights.append(jnp.exp2((scores - peak) * RATE).astype(BF16))
        peaks.append(jnp.broadcast_to(peak, (scores.shape[0], HEAD_DIM)))
    if len(parts) == 2:
        none = jnp.zeros((BLOCK, BLOCK), BF16)
        weights = [
            jnp.concatenate([weights[0], none], axis=1),
            jnp.concatenate([none, weights[1]], axis=1),
        ]
    weights = jnp.concatenate(weights, axis=0) if len(weights) == 2 else weights[0]
    peak = jnp.concatenate(peaks, axis=0) if len(peaks) == 2 else peaks[0]
    ones = jnp.ones((values.shape[0], HEAD_DIM), BF16)
    both = jnp.dot(weights, jnp.concatenate([values, ones], axis=1), preferred_element_type=F32)
    return peak, both[:, :HEAD_DIM], both[:, HEAD_DIM:]


def attend_all(windows):
    ahead = 2
    scores, terms = {}, []
    for at in range(len(windows) + ahead):
        if at < len(windows):
            scores[at] = raw_scores(*windows[at])
        if at >= ahead:
            terms.append(softmax_terms(scores.pop(at - ahead), windows[at - ahead][2]))
    return terms


def stack(parts):
    return tuple(jnp.concatenate(items, axis=0) for items in zip(*parts))


def merged(height, fine, coarse, scratch):
    rows = fine[0].shape[0]
    spread = []
    for which, part in enumerate(coarse):
        scratch[which, pl.ds(0, rows // 2, stride=2), :] = part
        scratch[which, pl.ds(1, rows // 2, stride=2), :] = part
        spread.append(scratch[which, pl.ds(0, rows), :])
    top = jnp.maximum(fine[0], spread[0])
    here = jnp.exp2((fine[0] - top) * RATE) * float(1 << height)
    there = jnp.exp2((spread[0] - top) * RATE)
    return (top, here * fine[1] + there * spread[1], here * fine[2] + there * spread[2])


def bias_row(pieces):
    total = sum(count for count, _ in pieces)
    lane = lax.broadcasted_iota(jnp.int32, (1, total), 1)
    row = jnp.zeros((1, total), F32)
    start = 0
    for count, allowed in pieces:
        if allowed is not None:
            inside = (lane >= start) & (lane < start + count)
            row = jnp.where(inside, jnp.where(allowed, 0.0, MASKED), row)
        start += count
    return row


def edge_flags(height, position, ctx_size):
    span = max(1, (1 << height) // 4)
    block = position // span
    return block >= 1, block + 1 < ctx_size // span


def head_windows(position, ctx_size, halving, admission, q, kv, left, right, thirds, fourths):
    everything = jnp.concatenate([kv, q], axis=1)
    levels = [everything]
    for _ in range(4):
        levels.append(pool(levels[-1], halving))
    q_at = [level[:, 2 * HEAD_DIM :] for level in levels]
    kv_at = [level[:, : 2 * HEAD_DIM] for level in levels]

    left0, right0 = left[0:128], right[0:128]
    left1 = jnp.concatenate([left[128:192], pool(left0, halving)], axis=0)
    right1 = jnp.concatenate([pool(right0, halving), right[128:192]], axis=0)
    left2 = jnp.concatenate([left[192:256], pool(left1, halving)], axis=0)
    right2 = jnp.concatenate([pool(right1, halving), right[192:256]], axis=0)

    def window(queries, pieces, admitted=None):
        rows = jnp.concatenate([piece for piece, _ in pieces], axis=0)
        bias = admitted
        if any(allowed is not None for _, allowed in pieces):
            edge = bias_row([(piece.shape[0], allowed) for piece, allowed in pieces])
            bias = edge if admitted is None else admitted + edge
        return queries, rows[:, :HEAD_DIM], rows[:, HEAD_DIM:], (bias,)

    def two_blocks(queries, rows, biases):
        return queries, rows[:, :HEAD_DIM], rows[:, HEAD_DIM:], biases

    has_left, has_right = edge_flags(4, position, ctx_size)
    is_right = position % 4 < 2
    mixed = (is_right & has_right) | (~is_right & has_left)
    pieces = []
    for chunks in (fourths[:3], fourths[3:]):
        pieces += list(zip(chunks, (has_left, has_right, mixed)))
    windows = [window(q_at[4], pieces)]

    has_left, has_right = edge_flags(3, position, ctx_size)
    odd = position % 2 == 1
    own = (odd & has_right) | (~odd & has_left)
    other = (odd & has_left) | (~odd & has_right)
    windows.append(window(q_at[3], [(thirds[0], own), (thirds[1], other), (thirds[2], other)]))

    has_left, has_right = edge_flags(2, position, ctx_size)
    windows.append(window(q_at[2], [(left2, has_left), (right2, has_right)], admission))

    q1, kv1 = q_at[1], kv_at[1]
    windows.append(window(q1[:128], [(left1, has_left), (kv1[128:], None)], admission))
    windows.append(window(q1[128:], [(kv1[:128], None), (right1, has_right)], admission))

    first = bias_row([(128, has_left), (256, None)])
    last = bias_row([(256, None), (128, has_right)])
    windows.append(two_blocks(q[:256], jnp.concatenate([left0, kv[:384]], axis=0), (first, None)))
    windows.append(two_blocks(q[256:], jnp.concatenate([kv[128:], right0], axis=0), (None, last)))
    return windows


def merge_windows(terms, scratch):
    peak, total, weight = terms[0]
    state = (peak, total * 16.0, weight * 16.0)
    for height, cut in ((3, slice(1, 2)), (2, slice(2, 3)), (1, slice(3, 5)), (0, slice(5, 7))):
        state = merged(height, stack(terms[cut]), state, scratch)
    return (state[1] / state[2]).astype(BF16)


SLOT_OFFSETS = [
    (-1, -1, -1, -1),
    (1, 1, 1, 1),
    (-2, 2, -2, 2),
    (-4, -4, -4, -4),
    (4, 4, 4, 4),
    (6, 6, -6, -6),
]
PASSED = 5
REACH = 7
CHUNKS = 8
AHEAD = 4
WEIGHT_CHUNKS = (0, 2, 4, 1, 3, 5, 3, 3, 5, 7)
CHUNK_HEADS = HEADS // CHUNKS


def by_turn(turn, table):
    value = table[3]
    for at in (2, 1, 0):
        value = jnp.where(turn == at, table[at], value)
    return value


def inverse(table):
    back = [0, 0, 0, 0]
    for turn, offset in enumerate(table):
        back[(turn + offset) % 4] = -offset
    return tuple(back)


def layer_kernel(ctx_size, with_weight, *refs):
    if with_weight:
        q_ref, k_ref, v_ref, w_ref, out_ref = refs[:5]
        refs = refs[5:]
        w_all, w_recv, w_send, w_core = refs[-4:]
    else:
        q_ref, k_ref, v_ref, out_ref = refs[:4]
        refs = refs[4:]
    (to_right, to_left, third, fourth, rims, thirds, fourths, pooled, their_thirds,
     their_pooled, their_fourths, scratch, att, halving, admission, send_sem,
     recv_sem, pass_send, pass_recv) = refs[:19]

    halving[...] = pooling_matrix()
    admission[...] = admission_bias()
    position = lax.axis_index("ctx")
    group = lax.axis_index("groups")
    turn = position % 4

    barrier = pltpu.get_barrier_semaphore()
    reach = ctx_size - 1 if with_weight else min(REACH, ctx_size - 1)
    for distance in range(1, reach + 1):
        for offset in (-distance, distance):
            peer = position + offset

            @pl.when((peer >= 0) & (peer < ctx_size))
            def _():
                pl.semaphore_signal(
                    barrier, inc=1, device_id={"ctx": peer}, device_id_type=pl.DeviceIdType.MESH
                )

    peers = jnp.minimum(position, reach) + jnp.minimum(ctx_size - 1 - position, reach)
    if with_weight:
        pl.semaphore_signal(
            barrier, inc=1, device_id={"groups": 1 - group}, device_id_type=pl.DeviceIdType.MESH
        )
        peers = peers + 1

    slots = [rims.at[0], rims.at[1], thirds] + [fourths.at[i] for i in range(3)]
    sources = [to_right, to_left, third] + [fourth] * 3
    passed = [thirds, pooled] + [fourths.at[i] for i in range(3)]
    passed_to = [their_thirds, their_pooled] + [their_fourths.at[i] for i in range(3)]
    sibling = position + 1 - 2 * (position % 2)
    givers = [position + by_turn(turn, table) for table in SLOT_OFFSETS]
    takers = [position + by_turn(turn, inverse(table)) for table in SLOT_OFFSETS]
    inside = lambda peer: (peer >= 0) & (peer < ctx_size)

    own_there = [inside(giver) for giver in givers]
    across = inside(position + 2 - 4 * (position % 2))
    send_there = [own_there[2], own_there[2]] + own_there[3:]
    pass_there = [across, across] + own_there[3:]

    pl.semaphore_wait(barrier, peers)

    for slot, there in zip(slots + passed_to, own_there + pass_there):

        @pl.when(jnp.logical_not(there))
        def _():
            slot[...] = jnp.zeros(slot.shape, BF16)

    def when(condition, action):
        if condition is None:
            action()
        else:
            pl.when(condition)(action)

    def slot_copy(chunk, which):
        heads = pl.ds(chunk * CHUNK_HEADS, CHUNK_HEADS)
        return pltpu.make_async_remote_copy(
            src_ref=sources[which].at[heads],
            dst_ref=slots[which].at[heads],
            send_sem=send_sem.at[chunk, which],
            recv_sem=recv_sem.at[chunk, which],
            device_id={"ctx": takers[which]},
            device_id_type=pl.DeviceIdType.MESH,
        )

    def pass_copy(chunk, which):
        heads = pl.ds(chunk * CHUNK_HEADS, CHUNK_HEADS)
        return pltpu.make_async_remote_copy(
            src_ref=passed[which].at[heads],
            dst_ref=passed_to[which].at[heads],
            send_sem=pass_send.at[chunk, which],
            recv_sem=pass_recv.at[chunk, which],
            device_id={"ctx": sibling},
            device_id_type=pl.DeviceIdType.MESH,
        )

    def forward(chunk):
        for which, there in enumerate(own_there):
            when(there, lambda which=which: slot_copy(chunk, which).wait_recv())
        lanes = []
        for at in range(CHUNK_HEADS):
            for which in range(2):
                lanes.append(rims[position % 2, chunk * CHUNK_HEADS + at, which])
        rows = jnp.concatenate(lanes, axis=1)
        eighth = jnp.concatenate(
            [
                pool(rows[192:256], halving),
                pool(pool(rows[128:192], halving), halving),
                pool(pool(pool(rows[0:128], halving), halving), halving),
            ],
            axis=0,
        )
        for at in range(CHUNK_HEADS):
            for which in range(2):
                start = (2 * at + which) * HEAD_DIM
                pooled[chunk * CHUNK_HEADS + at, which] = eighth[:, start : start + HEAD_DIM]
        for which, there in enumerate(send_there):
            when(there, lambda which=which: pass_copy(chunk, which).start())

    steps = []
    if with_weight:
        z = position // 4
        depth = ctx_size // 4
        partner = position + 2 - 4 * ((position // 2) % 2)

        def piece(shard, half, send, device):
            return pltpu.make_async_remote_copy(
                src_ref=w_all.at[shard, half],
                dst_ref=w_all.at[shard, half],
                send_sem=send,
                recv_sem=w_recv.at[shard, half],
                device_id=device,
                device_id_type=pl.DeviceIdType.MESH,
            )

        def to_x(shard):
            return piece(shard, group, w_send.at[0, shard], {"ctx": partner})

        def to_z(shard, way):
            kind = 1 if way > 0 else 2
            return piece(shard, group, w_send.at[kind, shard], {"ctx": position + 4 * way})

        def to_y(shard):
            return piece(shard, group, w_send.at[3, shard], {"groups": 1 - group})

        def to_core(shard, half, own):
            send = w_send.at[4, shard] if own else w_core.at[shard]
            return piece(shard, half, send, {"ctx": sibling})

        always = None
        can_go = {1: z + 1 < depth, -1: z >= 1}
        column = (position // 2) % 2
        rims_way = {1: column == 1, -1: column == 0}
        at_end = {1: z == depth - 1, -1: z == 0}
        by_z = {
            1: (z + 1 < depth) & ((column == 0) | (z + 1 != depth - 1)),
            -1: (z >= 1) & ((column == 1) | (z != 1)),
        }
        first = [(always, lambda: to_x(position))]
        for way in (1, -1):
            first.append((can_go[way], functools.partial(to_z, position, way)))
        first.append((always, lambda: to_core(position, group, True)))
        first.append((always, lambda: to_core(position, 1 - group, False)))
        steps.append([(always, None, first)])
        second = [(by_z[way], functools.partial(to_z, partner, way)) for way in (1, -1)]
        second.append((always, lambda: to_y(partner)))
        second.append((always, lambda: to_core(partner, group, True)))
        steps.append([(always, (partner, group), second)])
        late_steps = []
        for hops in range(1, depth):
            step, late = [], []
            for way in (1, -1):
                here = (z - hops * way >= 0) & (z - hops * way < depth)
                for base in (position, partner):
                    shard = base - 4 * hops * way
                    own = base is position
                    onward = can_go[way] if own else by_z[way]
                    sends = [
                        (onward, functools.partial(to_z, shard, way)),
                        (always, functools.partial(to_y, shard)),
                        (always, functools.partial(to_core, shard, group, True)),
                    ]
                    over_x = at_end[way] & rims_way[way]
                    if own:
                        pass_x = at_end[way] & jnp.logical_not(rims_way[way])
                        sends.append((pass_x, functools.partial(to_x, shard)))
                        step.append((here, (shard, group), sends))
                    else:
                        step.append((here & jnp.logical_not(over_x), (shard, group), sends))
                        late.append((here & over_x, (shard, group), sends[1:]))
            steps.append(step)
            late_steps.append(late)
        steps += late_steps
        for hops in range(depth):
            step = []
            for way in (1, -1):
                here = (z - hops * way >= 0) & (z - hops * way < depth)
                for base in (position, partner):
                    if hops == 0 and (way < 0 or base is position):
                        continue
                    shard = base - 4 * hops * way
                    sends = [(always, functools.partial(to_core, shard, 1 - group, False))]
                    step.append((here, (shard, 1 - group), sends))
            steps.append(step)

    def run_step(step):
        for here, awaited, sends in step:

            def act(awaited=awaited, sends=sends):
                if awaited is not None:
                    piece(*awaited, w_core.at[0], {"ctx": sibling}).wait_recv()
                for condition, copy in sends:
                    when(condition, lambda copy=copy: copy().start())

            when(here, act)

    def finish_step(step):
        for here, _, sends in step:

            def act(sends=sends):
                for condition, copy in sends:
                    when(condition, lambda copy=copy: copy().wait_send())

            when(here, act)

    if with_weight:
        w_all[position, 0] = w_ref[0:1024]
        w_all[position, 1] = w_ref[1024:2048]
        run_step(steps[0])

    def prepare(chunk, _):
        cols = CHUNK_HEADS * HEAD_DIM
        lanes = pl.ds(pl.multiple_of(chunk * cols, cols), cols)
        for which, ref in enumerate((k_ref, v_ref)):
            rows = ref[:, lanes]
            first = pool(rows, halving)
            second = pool(first, halving)
            eighth = pool(second, halving)
            sixteenth = pool(eighth, halving)
            for at in range(CHUNK_HEADS):
                head = chunk * CHUNK_HEADS + at
                cut = slice(at * HEAD_DIM, (at + 1) * HEAD_DIM)
                to_right[head, which, 0:128] = rows[384:512, cut]
                to_right[head, which, 128:192] = first[128:192, cut]
                to_right[head, which, 192:256] = second[0:64, cut]
                to_left[head, which, 0:128] = rows[0:128, cut]
                to_left[head, which, 128:192] = first[64:128, cut]
                to_left[head, which, 192:256] = second[64:128, cut]
                third[head, which] = eighth[:, cut]
                fourth[head, which] = sixteenth[:, cut]
        for which, taker in enumerate(takers):
            when(inside(taker), lambda which=which: slot_copy(chunk, which).start())
        return 0

    lax.fori_loop(0, AHEAD, prepare, 0)
    if with_weight:
        run_step(steps[1])
    forward(0)

    def one_chunk(chunk, _):
        @pl.when(chunk + AHEAD < CHUNKS)
        def _():
            prepare(chunk + AHEAD, 0)

        @pl.when(chunk + 1 < CHUNKS)
        def _():
            forward(chunk + 1)

        for which, there in enumerate(pass_there):
            when(there, lambda which=which: pass_copy(chunk, which).wait_recv())

        if with_weight:
            for at, step in enumerate(steps[2:]):
                pl.when(chunk == WEIGHT_CHUNKS[at])(functools.partial(run_step, step))
        windows = []
        for at in range(CHUNK_HEADS):
            head = chunk * CHUNK_HEADS + at
            lanes = pl.ds(pl.multiple_of(head * HEAD_DIM, HEAD_DIM), HEAD_DIM)
            pair = lambda ref: jnp.concatenate([ref[head, 0], ref[head, 1]], axis=1)
            windows.append(
                head_windows(
                    position,
                    ctx_size,
                    halving,
                    admission[...],
                    q_ref[:, lanes],
                    jnp.concatenate([k_ref[:, lanes], v_ref[:, lanes]], axis=1),
                    pair(rims.at[0]),
                    pair(rims.at[1]),
                    [pair(ref) for ref in (thirds, their_thirds, their_pooled)],
                    [pair(ref.at[i]) for ref in (fourths, their_fourths) for i in range(3)],
                )
            )
        count = len(windows[0])
        terms = attend_all([one[at] for at in range(count) for one in windows])
        for at in range(CHUNK_HEADS):
            head = chunk * CHUNK_HEADS + at
            lanes = pl.ds(pl.multiple_of(head * HEAD_DIM, HEAD_DIM), HEAD_DIM)
            att[:, lanes] = merge_windows(terms[at::CHUNK_HEADS], scratch.at[at])
        return 0

    lax.fori_loop(0, CHUNKS, one_chunk, 0)

    if with_weight:
        def project(at, _):
            for half in range(2):
                theirs = 2 * at + 1 - position % 2
                piece(theirs, half, w_core.at[0], {"ctx": sibling}).wait_recv()
            count = 2048
            weight = jnp.concatenate(
                [w_all[2 * at].reshape(count, 128), w_all[2 * at + 1].reshape(count, 128)], axis=1
            )
            result = jnp.dot(att[...], weight, preferred_element_type=F32)
            out_ref[:, pl.ds(pl.multiple_of(at * 256, 256), 256)] = result.astype(BF16)
            return 0

        lax.fori_loop(0, ctx_size // 2, project, 0)
        for step in steps:
            finish_step(step)
    else:
        out_ref[...] = att[...]

    def settle(chunk, _):
        for which, taker in enumerate(takers):
            when(inside(taker), lambda which=which: slot_copy(chunk, which).wait_send())
        for which, there in enumerate(send_there):
            when(there, lambda which=which: pass_copy(chunk, which).wait_send())
        return 0

    lax.fori_loop(0, CHUNKS, settle, 0)


def layer(ctx_size, queries, keys, values, weight=None):
    rows, width = queries.shape
    per_head = lambda *lead: pltpu.VMEM((*lead, HEAD_DIM), BF16)
    slots = len(SLOT_OFFSETS)
    scratch = [
        per_head(HEADS, 2, 256),
        per_head(HEADS, 2, 256),
        per_head(HEADS, 2, 64),
        per_head(HEADS, 2, 32),
        per_head(2, HEADS, 2, 256),
        per_head(HEADS, 2, 64),
        per_head(3, HEADS, 2, 32),
        per_head(HEADS, 2, 64),
        per_head(HEADS, 2, 64),
        per_head(HEADS, 2, 64),
        per_head(3, HEADS, 2, 32),
        pltpu.VMEM((CHUNK_HEADS, 3, rows, HEAD_DIM), F32),
        pltpu.VMEM((rows, width), BF16),
        pltpu.VMEM((BLOCK, 2 * BLOCK), BF16),
        pltpu.VMEM((BLOCK, 2 * BLOCK), F32),
        pltpu.SemaphoreType.DMA((CHUNKS, slots)),
        pltpu.SemaphoreType.DMA((CHUNKS, slots)),
        pltpu.SemaphoreType.DMA((CHUNKS, PASSED)),
        pltpu.SemaphoreType.DMA((CHUNKS, PASSED)),
    ]
    operands = [queries, keys, values]
    if weight is not None:
        operands.append(weight)
        scratch += [
            pltpu.VMEM((ctx_size, 2, weight.shape[0] // 2, weight.shape[1]), BF16),
            pltpu.SemaphoreType.DMA((ctx_size, 2)),
            pltpu.SemaphoreType.DMA((5, ctx_size)),
            pltpu.SemaphoreType.DMA((ctx_size,)),
        ]
    return pl.pallas_call(
        functools.partial(layer_kernel, ctx_size, weight is not None),
        in_specs=[pl.BlockSpec(memory_space=pltpu.VMEM)] * len(operands),
        out_specs=pl.BlockSpec(memory_space=pltpu.VMEM),
        out_shape=jax.ShapeDtypeStruct((rows, width), BF16),
        scratch_shapes=scratch,
        compiler_params=pltpu.CompilerParams(
            collective_id=0, has_side_effects=True, vmem_limit_bytes=56 << 20
        ),
        name="layer",
    )(*operands)


def per_device(query_vectors, key_vectors, value_vectors, out_weight):
    ctx_size = lax.axis_size("ctx")
    in_kernel = (
        out_weight.shape[1] == 128 and ctx_size == 16 and lax.axis_size("groups") == 2
    )
    if in_kernel:
        return layer(ctx_size, query_vectors, key_vectors, value_vectors, out_weight)
    weight = lax.all_gather(out_weight, "ctx", axis=1, tiled=True)
    attended = layer(ctx_size, query_vectors, key_vectors, value_vectors)
    return jnp.dot(attended, weight, preferred_element_type=F32).astype(BF16)


def solution(mesh):
    in_specs = (
        P(("groups", "ctx"), None),
        P(("groups", "ctx"), None),
        P(("groups", "ctx"), None),
        P(None, "ctx"),
    )
    out_specs = P(("groups", "ctx"), None)
    return jax.shard_map(
        per_device, mesh=mesh, in_specs=in_specs, out_specs=out_specs, check_vma=False
    )
```
